128 devices in a mesh: frame: 16 (over x, z), head: 8 (over y, core).
Axes of the slice: x: 4, y: 4, z: 4, core: 2. Of those that a mesh axis runs over, the one named last changes fastest.
Arguments:
- queries: bfloat16 [10240, 5120], P('frame', 'head'), may hold values from -30 to 30
- key_rows: bfloat16 [10240, 5120], P('frame', 'head'), may hold values from -3 to 3
- value_rows: bfloat16 [10240, 5120], P('frame', 'head'), may hold values from -6 to 6
- out_weight: bfloat16 [5120, 5120], P('head'), may hold values from -2.390625 to 2.390625
- band_start: int32 [16, 16], replicated, may hold values from 0 to 4
- band_width: int32 [16], replicated, may hold values from 1 to 5, as said below
Outputs:
- attn_out: bfloat16 [10240, 5120], P('frame', 'head')
The draws below stay inside these ranges and needn't reach their ends.
Inputs may be any that keep to these rules, and one draw needn't show every extreme that they name: band_width[0] is 5, band_width[1] is 2, every other entry lies in 1 to 2.
All inputs are finite; a program needn't handle non-finite values.
Results may differ from the reference program's by a relative error of at most 0.022.
Values may be sent and summed in bfloat16 or wider, within the bound.
No kernel may reach another device: no remote copies, remote signals or barrier semaphores. Data moves between devices by JAX's collectives and lax.ppermute only.
A program may use at most 128 MiB of HBM per device.

```python
import jax
import jax.numpy as jnp
from jax import lax

D = 5120
H = 40
HD = 128
BLOCK = 128
FT = 640
NB = 5
CAP = 2
FRAMES = 16
TOKENS = 10240
N_HEAD = 8


def draw_queries(key, part):
    key = jax.random.fold_in(key, 4)
    return jnp.clip(jax.random.normal(key, (TOKENS, H * HD), jnp.float32), -3.0, 3.0).astype(jnp.bfloat16)


def draw_key_rows(key, part):
    key = jax.random.fold_in(key, 3)
    return jnp.clip(jax.random.normal(key, (TOKENS, H * HD), jnp.float32), -3.0, 3.0).astype(jnp.bfloat16)


def draw_band_width(key, part):
    key = jax.random.fold_in(key, 5)
    distance = jnp.arange(FRAMES, dtype=jnp.int32)
    drawn = jax.random.randint(key, (FRAMES,), 1, CAP + 1, dtype=jnp.int32)
    return jnp.where(distance == 0, NB, jnp.where(distance == 1, CAP, drawn)).astype(jnp.int32)


def touch_ends(values, rng, least, top_value):
    dims = values.shape
    place = [jax.random.randint(jax.random.fold_in(rng, axis), (), 0, dims[axis]) for axis in range(len(dims))]
    values = values.at[tuple(place)].set(least)
    longest = dims.index(max(dims))
    place[longest] = (place[longest] + 1) % dims[longest]
    return values.at[tuple(place)].set(top_value)


def strengthened(array, key, source, target, parts, factor):
    owner, partner = [(jnp.arange(array.shape[dim]) // (array.shape[dim] // parts)).reshape([-1 if axis == dim else 1 for axis in range(array.ndim)]) for dim in (source, target)]
    chosen = jax.random.permutation(key, parts)[partner]
    strong = (owner == chosen) | (owner == (partner + parts // 2) % parts)
    return jnp.where(strong, factor * array, array)


def block_levels(stream_key, dims, shards, smallest, top_value):
    gain, own = 1.0, jax.random.fold_in(stream_key, 6)
    for axis_at, parts in shards:
        heights = jnp.exp(jax.random.uniform(jax.random.fold_in(own, axis_at), (parts,), jnp.float32, smallest / len(shards), top_value / len(shards)))
        gain = gain * jnp.repeat(heights, dims[axis_at] // parts).reshape([-1 if axis == axis_at else 1 for axis in range(len(dims))])
    return gain


def normal_values(key, shape, deviation, reach, shards=(), kind=jnp.bfloat16):
    array = deviation * jax.random.normal(key, shape, jnp.float32)
    if shards:
        array = array * block_levels(key, shape, shards, -0.22, 0.18)
    return jnp.clip(array, -reach, reach).astype(kind)


def bell_draw_with(rng, shape, spread, reach, pieces, heavy, held_as=jnp.bfloat16):
    result = spread * jax.random.normal(rng, shape, jnp.float32)
    if pieces:
        result = result * block_levels(rng, shape, pieces, -0.22, 0.18)
    return jnp.clip(strengthened(result, jax.random.fold_in(rng, 3), *heavy), -reach, reach).astype(held_as)


def setup_inputs(seed: int = 0) -> dict:
    streams_of = jax.random.split(jax.random.key(seed), 7)
    return {
        "queries": draw_queries(jax.random.fold_in(streams_of[6], 71), 0),
        "key_rows": draw_key_rows(jax.random.fold_in(streams_of[6], 71), 0),
        "value_rows": normal_values(streams_of[2], (TOKENS, H * HD), 1.0, 6.0, ((0, 16), (1, 8))),
        "out_weight": bell_draw_with(streams_of[3], (H * HD, D), 0.4, 2.390625, ((0, 8),), (0, 1, 8, 2.0)),
        "band_start": touch_ends(jax.random.randint(streams_of[4], (FRAMES, FRAMES), 0, NB), jax.random.fold_in(streams_of[4], 1), 0, NB - 1).astype(jnp.int32),
        "band_width": draw_band_width(jax.random.fold_in(streams_of[6], 71), 0),
    }


def reference(queries, key_rows, value_rows, out_weight, band_start, band_width):
    scaling = HD ** -0.5
    query_heads = queries.reshape(TOKENS, H, HD).transpose(1, 0, 2)
    key_heads = key_rows.reshape(TOKENS, H, HD).transpose(1, 0, 2)
    value_heads = value_rows.reshape(TOKENS, H, HD).transpose(1, 0, 2)
    key_index = jnp.arange(TOKENS, dtype=jnp.int32)
    key_frame = key_index // FT
    key_block = (key_index % FT) // BLOCK

    def frame_allow(frame):
        first_block = jnp.take(band_start[frame], key_frame)
        band_len = jnp.take(band_width, jnp.abs(frame - key_frame))
        return (key_frame == frame) | (jnp.mod(key_block - first_block, NB) < band_len)

    masks = lax.map(frame_allow, jnp.arange(FRAMES, dtype=jnp.int32))

    def one_head(operands):
        query_one, key_one, value_one = operands

        def one_frame(frame):
            query_part = lax.dynamic_slice_in_dim(query_one, frame * FT, FT, 0)
            scores = jnp.dot(query_part, key_one.T, preferred_element_type=jnp.float32) * scaling
            allowed = masks[frame]
            scores = jnp.where(allowed[None, :], scores, -jnp.inf)
            maxima = jnp.max(scores, axis=1, keepdims=True)
            weights_now = jnp.exp(scores - maxima)
            totals = jnp.sum(weights_now, axis=1, keepdims=True)
            mixed = jnp.dot(weights_now.astype(jnp.bfloat16), value_one, preferred_element_type=jnp.float32)
            return (mixed / totals).astype(jnp.bfloat16)

        return lax.map(one_frame, jnp.arange(FRAMES, dtype=jnp.int32)).reshape(TOKENS, HD)

    attended = lax.map(one_head, (query_heads, key_heads, value_heads))
    attended = attended.transpose(1, 0, 2).reshape(TOKENS, H * HD)
    group = H // N_HEAD
    grouped_attn = attended.reshape(TOKENS, N_HEAD, group * HD).transpose(1, 0, 2)
    grouped_weight = out_weight.reshape(N_HEAD, group * HD, D)

    def add_group(running, operands):
        partial_value = jnp.dot(operands[0], operands[1], preferred_element_type=jnp.float32).astype(jnp.bfloat16)
        partial_value = lax.optimization_barrier(partial_value).astype(jnp.float32)
        return running + partial_value, None

    running, unused = lax.scan(add_group, jnp.zeros((TOKENS, D), jnp.float32), (grouped_attn, grouped_weight))
    return running.astype(jnp.bfloat16)
```

```python
import functools

import jax
import jax.numpy as jnp
from jax import lax
from jax.experimental import pallas as pl
from jax.experimental.pallas import tpu as pltpu
from jax.sharding import PartitionSpec as P

HD = 128
BLOCK = 128
NB = 5
FT = 640
FRAMES = 16
SIDE = 4
CHUNK = 16
ROWS = 128
LOG2_SCALE = 1.4426950408889634 / HD**0.5
NT = (((1,), (1,)), ((), ()))
NN = (((1,), (0,)), ((), ()))
BOTH = ("frame", "head")


def pairs(move):
    out = []
    for i in range(128):
        frame, head = divmod(i, 8)
        x, z, y, c = move(*divmod(frame, 4), *divmod(head, 2))
        out.append((i, (x % 4 * 4 + z % 4) * 8 + y % 4 * 2 + c))
    return out


def line_shift(v, s):
    return lax.ppermute(v, BOTH, pairs(lambda x, z, y, c: (x, z + s, y, c) if c == 0 else (x + s, z, y, c)))


def cross_shift(v, s):
    return lax.ppermute(v, BOTH, pairs(lambda x, z, y, c: (x + s, z, y, c) if c == 0 else (x, z + s, y, c)))


def y_shift(v, s):
    return lax.ppermute(v, BOTH, pairs(lambda x, z, y, c: (x, z, y + s, c)))


def core_swap(v):
    return lax.ppermute(v, BOTH, pairs(lambda x, z, y, c: (x, z, y, 1 - c)))


def attend_kernel(qid, kid, bs, bw, q_ref, g0, g1, g2, g3, o_ref, kc, vc, acc, mx):
    a = qid[pl.program_id(0)]

    def place(n):
        return pl.ds(pl.multiple_of(n * BLOCK, BLOCK), BLOCK)

    n = 0
    for d, group in enumerate((g0, g1, g2, g3)):

        def pack(s, n, d=d, group=group):
            b = kid[d * SIDE + s]
            own = a == b
            start = jnp.where(own, 0, bs[a * FRAMES + b])
            width = jnp.where(own, NB, bw[jnp.abs(a - b)])

            def one(t, n):
                at = start + t
                rows = place(jnp.where(at >= NB, at - NB, at))
                kc[place(n), :] = group[s, 0, rows, :]
                vc[place(n), 0:HD] = group[s, 1, rows, :]
                vc[place(n), HD:] = (lax.broadcasted_iota(jnp.int32, (BLOCK, HD), 1) == 0).astype(jnp.bfloat16)
                return n + 1

            return lax.fori_loop(0, width, one, n)

        n = lax.fori_loop(0, SIDE, pack, n)
    steps = (n + CHUNK - 1) // CHUNK

    def fill(j, carry):
        kc[place(j), :] = kc[0:BLOCK, :]
        vc[place(j), :] = jnp.zeros((BLOCK, 2 * HD), jnp.bfloat16)
        return carry

    lax.fori_loop(n, steps * CHUNK, fill, 0)
    acc[...] = jnp.zeros_like(acc)
    mx[...] = jnp.full_like(mx, -1e30)

    def step(j, carry):
        keys = pl.ds(pl.multiple_of(j * CHUNK * BLOCK, CHUNK * BLOCK), CHUNK * BLOCK)
        kk, vv = kc[keys, :], vc[keys, :]
        for r in range(FT // ROWS):
            rows = slice(r * ROWS, (r + 1) * ROWS)
            scores = lax.dot_general(q_ref[0, rows, :], kk, NT, preferred_element_type=jnp.float32)
            old = mx[rows, :]
            new = jnp.maximum(old, jnp.max(scores, axis=1, keepdims=True))
            mx[rows, :] = new
            top = new * LOG2_SCALE
            probs = jnp.exp2(scores * LOG2_SCALE - top[:, 0:1]).astype(jnp.bfloat16)
            factor = jnp.exp2(old * LOG2_SCALE - top)
            acc[rows, :] = acc[rows, :] * factor[:, 0:1] + lax.dot_general(
                probs, vv, NN, preferred_element_type=jnp.float32
            )
        return carry

    lax.fori_loop(0, steps, step, 0)
    o_ref[0] = (acc[:, 0:HD] / acc[:, HD : HD + 1]).astype(jnp.bfloat16)


def attend(qid, kid, bs, bw, q, groups):
    items = q.shape[0]
    most = -(-(NB + 2 * (FRAMES - 1)) // CHUNK) * CHUNK * BLOCK
    whole = pl.BlockSpec((SIDE, 2, FT, HD), lambda i, *_: (0, 0, 0, 0))
    item = pl.BlockSpec((1, FT, HD), lambda i, *_: (i, 0, 0))
    return pl.pallas_call(
        attend_kernel,
        grid_spec=pltpu.PrefetchScalarGridSpec(
            num_scalar_prefetch=4,
            grid=(items,),
            in_specs=[item] + [whole] * 4,
            out_specs=item,
            scratch_shapes=[
                pltpu.VMEM((most, HD), jnp.bfloat16),
                pltpu.VMEM((most, 2 * HD), jnp.bfloat16),
                pltpu.VMEM((FT, 2 * HD), jnp.float32),
                pltpu.VMEM((FT, HD), jnp.float32),
            ],
        ),
        out_shape=jax.ShapeDtypeStruct((items, FT, HD), jnp.bfloat16),
        compiler_params=pltpu.CompilerParams(vmem_limit_bytes=48 << 20),
        cost_estimate=pl.CostEstimate(
            flops=items * 4 * FT * HD * 28 * BLOCK, bytes_accessed=6 << 20, transcendentals=items * FT * 28 * BLOCK
        ),
        name="attend",
    )(qid, kid, bs, bw, q, *groups)


def project_kernel(order, pos, o0, o1, o2, o3, o4, w_ref, y_ref, att):
    @pl.when(pl.program_id(0) == 0)
    def _():
        for s, o in enumerate((o0, o1, o2, o3)):
            head = lax.rem(pos[0] + s, SIDE)
            att[:, pl.ds(pl.multiple_of(head * HD, HD), HD)] = o[...]
        att[:, 4 * HD :] = o4[...]

    y_ref[0] = jnp.dot(att[...], w_ref[...], preferred_element_type=jnp.float32).astype(jnp.bfloat16)


def project(order, pos, outs, weight):
    count = order.shape[0]
    width = weight.shape[1] // 8
    whole = pl.BlockSpec((FT, HD), lambda i, *_: (0, 0))
    return pl.pallas_call(
        project_kernel,
        grid_spec=pltpu.PrefetchScalarGridSpec(
            num_scalar_prefetch=2,
            grid=(count,),
            in_specs=[whole] * 5 + [pl.BlockSpec((5 * HD, width), lambda i, order, pos: (0, order[i]))],
            out_specs=pl.BlockSpec((1, FT, width), lambda i, *_: (i, 0, 0)),
            scratch_shapes=[pltpu.VMEM((FT, 5 * HD), jnp.bfloat16)],
        ),
        out_shape=jax.ShapeDtypeStruct((count, FT, width), jnp.bfloat16),
        compiler_params=pltpu.CompilerParams(vmem_limit_bytes=48 << 20),
        cost_estimate=pl.CostEstimate(
            flops=2 * count * FT * 5 * HD * width, bytes_accessed=count * 2 * FT * width * 2, transcendentals=0
        ),
        name="project",
    )(order, pos, *outs, weight)


def add(*terms):
    total = terms[0].astype(jnp.float32)
    for t in terms[1:]:
        total = total + t.astype(jnp.float32)
    return total.astype(jnp.bfloat16)


def shards(queries, key_rows, value_rows, out_weight, band_start, band_width):
    frame, head = lax.axis_index("frame"), lax.axis_index("head")
    x, z = frame // SIDE, frame % SIDE
    y, core = head // 2, head % 2
    line = jnp.where(core == 0, z, x)
    ring = jnp.arange(SIDE, dtype=jnp.int32)
    line_frames = jnp.where(core == 0, x * SIDE + (z - ring) % SIDE, (x - ring) % SIDE * SIDE + z)
    back, slot = ring[:, None], ring[None, :]
    all_frames = jnp.where(
        core == 0,
        (x - back) % SIDE * SIDE + (z - slot) % SIDE,
        (x - slot) % SIDE * SIDE + (z - back) % SIDE,
    ).reshape(-1)
    bs, bw = band_start.reshape(-1), band_width

    def columns(v, h):
        return lax.dynamic_slice_in_dim(v, h * HD, HD, 1)

    k4, v4 = key_rows[:, 4 * HD :], value_rows[:, 4 * HD :]
    got = []
    for s in range(SIDE):
        h = (line + s) % SIDE
        piece = jnp.stack([columns(queries, h), columns(key_rows, h), columns(value_rows, h), k4, v4])
        got.append(piece if s == 0 else line_shift(piece, s))
    q_main = jnp.stack([g[0] for g in got])
    main = [jnp.stack([g[1:3] for g in got])]
    last = [jnp.stack([g[3:5] for g in got])]

    main_1, main_3 = cross_shift(main[0], 1), cross_shift(main[0], 3)
    last_1, last_3 = cross_shift(last[0], 1), cross_shift(last[0], 3)
    main += [main_1, cross_shift(main_1, 1), main_3]
    last += [last_1, cross_shift(last_3, 3), last_3]

    o_main = attend(line_frames, all_frames, bs, bw, q_main, main)
    o_last = attend(frame[None], all_frames, bs, bw, queries[None, :, 4 * HD :], last)

    outs = [o_main[0]] + [line_shift(o_main[s], SIDE - s) for s in range(1, SIDE)] + [o_last[0]]

    far = (y + jnp.array([2, 1, 3, 0], jnp.int32)) % SIDE * 2
    given = core_swap(project(far + 1 - core, line[None], outs, out_weight))
    kept = project(far + core, line[None], outs, out_weight)
    two, up, down, own = [add(kept[i], given[i]) for i in range(4)]
    half = FT // 2
    from_down, from_up = y_shift(two[:half], 1), y_shift(two[half:], 3)
    up = jnp.concatenate([add(up[:half], from_down), up[half:]])
    down = jnp.concatenate([down[:half], add(down[half:], from_up)])
    return add(own, y_shift(up, 1), y_shift(down, 3))


def solution(mesh):
    return jax.shard_map(
        shards,
        mesh=mesh,
        in_specs=(
            P("frame", "head"),
            P("frame", "head"),
            P("frame", "head"),
            P("head", None),
            P(),
            P(),
        ),
        out_specs=P("frame", "head"),
        check_vma=False,
    )
```

```python
import functools

import jax
import jax.numpy as jnp
from jax import lax
from jax.experimental import pallas as pl
from jax.experimental.pallas import tpu as pltpu
from jax.sharding import PartitionSpec as P

HD = 128
BLOCK = 128
NB = 5
FT = 640
FRAMES = 16
SIDE = 4
ROWS = 128
LOG2_SCALE = 1.4426950408889634 / HD**0.5
NT = (((1,), (1,)), ((), ()))
NN = (((1,), (0,)), ((), ()))
BOTH = ("frame", "head")


def pairs(move):
    out = []
    for i in range(128):
        frame, head = divmod(i, 8)
        x, z, y, c = move(*divmod(frame, 4), *divmod(head, 2))
        out.append((i, (x % 4 * 4 + z % 4) * 8 + y % 4 * 2 + c))
    return out


def line_shift(v, s):
    return lax.ppermute(v, BOTH, pairs(lambda x, z, y, c: (x, z + s, y, c) if c == 0 else (x + s, z, y, c)))


def cross_shift(v, s):
    return lax.ppermute(v, BOTH, pairs(lambda x, z, y, c: (x + s, z, y, c) if c == 0 else (x, z + s, y, c)))


def y_shift(v, s):
    return lax.ppermute(v, BOTH, pairs(lambda x, z, y, c: (x, z, y + s, c)))


def core_swap(v):
    return lax.ppermute(v, BOTH, pairs(lambda x, z, y, c: (x, z, y, 1 - c)))


def pick_kernel(count, pos, *refs):
    arrays, outs, sems = refs[:count], refs[-5:-1], refs[-1]
    copies = []
    for s in range(SIDE):
        head = lax.rem(pos[0] + s, SIDE)
        for j, array in enumerate(arrays):
            source = array.at[:, pl.ds(pl.multiple_of(head * HD, HD), HD)]
            copies.append(pltpu.make_async_copy(source, outs[s].at[j], sems.at[s * count + j]))
    for copy in copies:
        copy.start()
    for copy in copies:
        copy.wait()


def pick(pos, *arrays):
    count = len(arrays)
    return pl.pallas_call(
        functools.partial(pick_kernel, count),
        grid_spec=pltpu.PrefetchScalarGridSpec(
            num_scalar_prefetch=1,
            grid=(1,),
            in_specs=[pl.BlockSpec(memory_space=pl.ANY)] * count,
            out_specs=[pl.BlockSpec(memory_space=pl.ANY)] * SIDE,
            scratch_shapes=[pltpu.SemaphoreType.DMA((SIDE * count,))],
        ),
        out_shape=[jax.ShapeDtypeStruct((count, FT, HD), jnp.bfloat16)] * SIDE,
        name="pick",
    )(pos, *arrays)


def last_head_kernel(after, keys, values, out, sems):
    del after
    copies = [
        pltpu.make_async_copy(array.at[:, 4 * HD :], out.at[j], sems.at[j]) for j, array in enumerate((keys, values))
    ]
    for copy in copies:
        copy.start()
    for copy in copies:
        copy.wait()


def last_head(after, keys, values):
    return pl.pallas_call(
        last_head_kernel,
        in_specs=[pl.BlockSpec(memory_space=pl.ANY)] * 3,
        out_specs=pl.BlockSpec(memory_space=pl.ANY),
        scratch_shapes=[pltpu.SemaphoreType.DMA((2,))],
        out_shape=jax.ShapeDtypeStruct((2, FT, HD), jnp.bfloat16),
        name="last_head",
    )(after, keys, values)


def block_rows(n):
    return pl.ds(pl.multiple_of(n * BLOCK, BLOCK), BLOCK)


def band_kernel(qid, kid, bs, group, *outs):
    for s in range(SIDE):
        for i, out in enumerate(outs):
            first = bs[qid[i] * FRAMES + kid[s]]
            second = jnp.where(first == NB - 1, 0, first + 1)
            for j in range(2):
                out[s, j, 0:BLOCK, :] = group[s, j, block_rows(first), :]
                out[s, j, BLOCK:, :] = group[s, j, block_rows(second), :]


def bands(qid, kid, bs, group):
    shape = (SIDE, 2, 2 * BLOCK, HD)
    return pl.pallas_call(
        band_kernel,
        grid_spec=pltpu.PrefetchScalarGridSpec(
            num_scalar_prefetch=3,
            grid=(1,),
            in_specs=[pl.BlockSpec(group.shape, lambda i, *_: (0, 0, 0, 0))],
            out_specs=[pl.BlockSpec(shape, lambda i, *_: (0, 0, 0, 0))] * 3,
        ),
        out_shape=[jax.ShapeDtypeStruct(shape, jnp.bfloat16)] * 3,
        name="bands",
    )(qid, kid, bs, group)


def attend_kernel(kinds, sizes, resumed, finished, qid, kid, bs, bw, q_ref, *refs):
    groups, refs = refs[: len(kinds)], refs[len(kinds) :]
    if resumed:
        acc_in, mx_in, refs = refs[0], refs[1], refs[2:]
    if finished:
        o_ref, kc, vc = refs
    else:
        acc_out, mx_out, kc, vc = refs
    a = qid[pl.program_id(0)]

    n = 0
    for d, (group, kind) in enumerate(zip(groups, kinds)):

        def pack(s, n, d=d, group=group, kind=kind):
            b = kid[d * SIDE + s]
            own = a == b
            start = jnp.where(own, 0, bs[a * FRAMES + b])
            width = jnp.where(own, NB, bw[jnp.abs(a - b)])

            def one(t, n):
                at = start + t
                at = t if kind == "band" else jnp.where(at >= NB, at - NB, at)
                kc[block_rows(n), :] = group[s, 0, block_rows(at), :]
                vc[block_rows(n), 0:HD] = group[s, 1, block_rows(at), :]
                vc[block_rows(n), HD:] = (lax.broadcasted_iota(jnp.int32, (BLOCK, HD), 1) == 0).astype(jnp.bfloat16)
                return n + 1

            return lax.fori_loop(0, width, one, n)

        n = lax.fori_loop(0, SIDE, pack, n)

    def attend_to(size):
        def fill(j, carry):
            kc[block_rows(j), :] = kc[0:BLOCK, :]
            vc[block_rows(j), :] = jnp.zeros((BLOCK, 2 * HD), jnp.bfloat16)
            return carry

        lax.fori_loop(n, size, fill, 0)
        kk, vv = kc[0 : size * BLOCK, :], vc[0 : size * BLOCK, :]
        for r in range(FT // ROWS):
            rows = slice(r * ROWS, (r + 1) * ROWS)
            scores = lax.dot_general(q_ref[0, rows, :], kk, NT, preferred_element_type=jnp.float32)
            new = jnp.max(scores, axis=1, keepdims=True)
            if resumed:
                old = mx_in[0, rows, :]
                new = jnp.maximum(old[:, 0:1], new)
            probs = jnp.exp2(scores * LOG2_SCALE - new * LOG2_SCALE).astype(jnp.bfloat16)
            mixed = lax.dot_general(probs, vv, NN, preferred_element_type=jnp.float32)
            if resumed:
                mixed = mixed + acc_in[0, rows, :] * jnp.exp2((old[:, 0:1] - new) * LOG2_SCALE)
            if finished:
                o_ref[0, rows, :] = (mixed[:, 0:HD] / mixed[:, HD : HD + 1]).astype(jnp.bfloat16)
            else:
                acc_out[0, rows, :] = mixed
                mx_out[0, rows, :] = jnp.broadcast_to(new, (ROWS, HD))

    for least, size in zip((-1,) + sizes[:-1], sizes):

        @pl.when((n > least) & (n <= size))
        def _(size=size):
            attend_to(size)


def attend(qid, kid, bs, bw, q, groups, sizes, state=None, finished=False):
    items = q.shape[0]
    kinds = tuple("whole" if g.shape[2] == FT else "band" for g in groups)
    item = pl.BlockSpec((1, FT, HD), lambda i, *_: (i, 0, 0))
    wide = pl.BlockSpec((1, FT, 2 * HD), lambda i, *_: (i, 0, 0))
    whole = [pl.BlockSpec(g.shape, lambda i, *_: (0, 0, 0, 0)) for g in groups]
    state = state or ()
    most = sizes[-1] * BLOCK
    keys = (sizes[0] + sizes[-1]) // 2 * BLOCK
    if finished:
        out_specs, out_shape = item, jax.ShapeDtypeStruct((items, FT, HD), jnp.bfloat16)
    else:
        out_specs = [wide, item]
        out_shape = [
            jax.ShapeDtypeStruct((items, FT, 2 * HD), jnp.float32),
            jax.ShapeDtypeStruct((items, FT, HD), jnp.float32),
        ]
    return pl.pallas_call(
        functools.partial(attend_kernel, kinds, sizes, bool(state), finished),
        grid_spec=pltpu.PrefetchScalarGridSpec(
            num_scalar_prefetch=4,
            grid=(items,),
            in_specs=[item] + whole + ([wide, item] if state else []),
            out_specs=out_specs,
            scratch_shapes=[pltpu.VMEM((most, HD), jnp.bfloat16), pltpu.VMEM((most, 2 * HD), jnp.bfloat16)],
        ),
        out_shape=out_shape,
        compiler_params=pltpu.CompilerParams(vmem_limit_bytes=40 << 20),
        cost_estimate=pl.CostEstimate(
            flops=items * 4 * FT * HD * keys, bytes_accessed=8 << 20, transcendentals=items * FT * keys
        ),
        name="attend",
    )(qid, kid, bs, bw, q, *groups, *state)


def project_kernel(order, pos, o0, o1, o2, o3, o4, w_ref, y_ref, att):
    @pl.when(pl.program_id(0) == 0)
    def _():
        for s, o in enumerate((o0, o1, o2, o3)):
            head = lax.rem(pos[0] + s, SIDE)
            att[:, pl.ds(pl.multiple_of(head * HD, HD), HD)] = o[...]
        att[:, 4 * HD :] = o4[...]

    y_ref[0] = jnp.dot(att[...], w_ref[...], preferred_element_type=jnp.float32).astype(jnp.bfloat16)


def project(order, pos, outs, weight):
    count = order.shape[0]
    width = weight.shape[1] // 8
    whole = pl.BlockSpec((FT, HD), lambda i, *_: (0, 0))
    return pl.pallas_call(
        project_kernel,
        grid_spec=pltpu.PrefetchScalarGridSpec(
            num_scalar_prefetch=2,
            grid=(count,),
            in_specs=[whole] * 5 + [pl.BlockSpec((5 * HD, width), lambda i, order, pos: (0, order[i]))],
            out_specs=pl.BlockSpec((1, FT, width), lambda i, *_: (i, 0, 0)),
            scratch_shapes=[pltpu.VMEM((FT, 5 * HD), jnp.bfloat16)],
        ),
        out_shape=jax.ShapeDtypeStruct((count, FT, width), jnp.bfloat16),
        compiler_params=pltpu.CompilerParams(vmem_limit_bytes=48 << 20),
        cost_estimate=pl.CostEstimate(
            flops=2 * count * FT * 5 * HD * width, bytes_accessed=count * 2 * FT * width * 2, transcendentals=0
        ),
        name="project",
    )(order, pos, *outs, weight)


def add(*terms):
    total = terms[0].astype(jnp.float32)
    for t in terms[1:]:
        total = total + t.astype(jnp.float32)
    return total.astype(jnp.bfloat16)


def shards(queries, key_rows, value_rows, out_weight, band_start, band_width):
    frame, head = lax.axis_index("frame"), lax.axis_index("head")
    x, z = frame // SIDE, frame % SIDE
    y, core = head // 2, head % 2
    line = jnp.where(core == 0, z, x)
    ring = jnp.arange(SIDE, dtype=jnp.int32)

    def frames_at(cross, along):
        return jnp.where(
            core == 0,
            (x - cross) % SIDE * SIDE + (z - along) % SIDE,
            (x - along) % SIDE * SIDE + (z - cross) % SIDE,
        )

    f0, f1, f2, f3 = [frames_at(d, ring) for d in range(SIDE)]
    bs, bw = band_start.reshape(-1), band_width

    pieces = pick(line[None], queries, key_rows, value_rows)
    got = [pieces[0]] + [line_shift(pieces[s], s) for s in range(1, SIDE)]
    q_main = jnp.stack([g[0] for g in got])
    main_0 = jnp.stack([g[1:3] for g in got])

    main_1, main_3 = cross_shift(main_0, 1), cross_shift(main_0, 3)
    main_2 = jnp.concatenate([cross_shift(main_1[:2], 1), cross_shift(main_3[2:], 3)])

    mine = last_head(main_3, key_rows, value_rows)
    last_0 = jnp.stack([mine] + [line_shift(mine, s) for s in range(1, SIDE)])
    sent = bands(frames_at(-ring[1:], 0), f0, bs, last_0)
    last_1, last_2, last_3 = [cross_shift(sent[s - 1], s) for s in range(1, SIDE)]

    state = attend(f0, f0, bs, bw, q_main, [main_0], (8, 10, 11))
    state = attend(f0, jnp.concatenate([f1, f3]), bs, bw, q_main, [main_1, main_3], (8, 10, 12, 14, 16), state)
    o_main = attend(f0, f2, bs, bw, q_main, [main_2], (4, 6, 8), state, True)
    q_last = queries[None, :, 4 * HD :]
    state = attend(frame[None], f0, bs, bw, q_last, [last_0], (8, 10, 11))
    o_last = attend(
        frame[None], jnp.concatenate([f1, f2, f3]), bs, bw, q_last, [last_1, last_2, last_3],
        (12, 14, 16, 18, 20, 22, 24), state, True,
    )

    outs = [o_main[0]] + [line_shift(o_main[s], SIDE - s) for s in range(1, SIDE)] + [o_last[0]]

    def summed(ahead):
        target = (y + jnp.array(ahead, jnp.int32)) % SIDE * 2
        given = core_swap(project(target + 1 - core, line[None], outs, out_weight))
        kept = project(target + core, line[None], outs, out_weight)
        return [add(kept[i], given[i]) for i in range(len(ahead))]

    half = FT // 2
    (two,) = summed([2])
    from_down, from_up = y_shift(two[:half], 1), y_shift(two[half:], 3)
    up, down, own = summed([1, 3, 0])
    plain_up, plain_down = y_shift(up[half:], 1), y_shift(down[:half], 3)
    more_up, more_down = y_shift(add(up[:half], from_down), 1), y_shift(add(down[half:], from_up), 3)
    return jnp.concatenate([add(own[:half], more_up, plain_down), add(own[half:], plain_up, more_down)])


def solution(mesh):
    return jax.shard_map(
        shards,
        mesh=mesh,
        in_specs=(
            P("frame", "head"),
            P("frame", "head"),
            P("frame", "head"),
            P("head", None),
            P(),
            P(),
        ),
        out_specs=P("frame", "head"),
        check_vma=False,
    )
```

```python
import functools

import jax
import jax.numpy as jnp
from jax import lax
from jax.experimental import pallas as pl
from jax.experimental.pallas import tpu as pltpu
from jax.sharding import PartitionSpec as P

HD = 128
BLOCK = 128
NB = 5
FT = 640
FRAMES = 16
SIDE = 4
ROWS = 128
LOG2_SCALE = 1.4426950408889634 / HD**0.5
NT = (((1,), (1,)), ((), ()))
NN = (((1,), (0,)), ((), ()))
BOTH = ("frame", "head")


def pairs(move):
    out = []
    for i in range(128):
        frame, head = divmod(i, 8)
        x, z, y, c = move(*divmod(frame, 4), *divmod(head, 2))
        out.append((i, (x % 4 * 4 + z % 4) * 8 + y % 4 * 2 + c))
    return out


def line_shift(v, s):
    return lax.ppermute(v, BOTH, pairs(lambda x, z, y, c: (x, z + s, y, c) if c == 0 else (x + s, z, y, c)))


def cross_shift(v, s):
    return lax.ppermute(v, BOTH, pairs(lambda x, z, y, c: (x + s, z, y, c) if c == 0 else (x, z + s, y, c)))


def y_shift(v, s):
    return lax.ppermute(v, BOTH, pairs(lambda x, z, y, c: (x, z, y + s, c)))


def core_swap(v):
    return lax.ppermute(v, BOTH, pairs(lambda x, z, y, c: (x, z, y, 1 - c)))


ANY = pl.BlockSpec(memory_space=pl.ANY)
VMEM = pl.BlockSpec(memory_space=pltpu.VMEM)
LIMIT = 20 << 20


def fence_kernel(*refs):
    del refs


def fence(values, *after):
    count = len(values)
    return pl.pallas_call(
        fence_kernel,
        in_specs=[ANY] * (count + len(after)),
        out_specs=[ANY] * count,
        out_shape=[jax.ShapeDtypeStruct(v.shape, v.dtype) for v in values],
        input_output_aliases={i: i for i in range(count)},
        name="fence",
    )(*values, *after)


def pick_kernel(pos, q_ref, k_ref, v_ref, *outs):
    for s, out in enumerate(outs):
        head = lax.rem(pos[0] + s, SIDE)
        columns = pl.ds(pl.multiple_of(head * HD, HD), HD)
        out[0] = q_ref[:, columns]
        out[1] = k_ref[:, columns]
        out[2] = v_ref[:, columns]
        out[3] = k_ref[:, 4 * HD :]
        out[4] = v_ref[:, 4 * HD :]


def pick(pos, queries, keys, values):
    return pl.pallas_call(
        pick_kernel,
        in_specs=[pl.BlockSpec(memory_space=pltpu.SMEM)] + [VMEM] * 3,
        out_specs=[VMEM] * SIDE,
        out_shape=[jax.ShapeDtypeStruct((5, FT, HD), jnp.bfloat16)] * SIDE,
        compiler_params=pltpu.CompilerParams(vmem_limit_bytes=LIMIT),
        name="pick",
    )(pos, queries, keys, values)


def block_rows(n):
    return pl.ds(pl.multiple_of(n * BLOCK, BLOCK), BLOCK)


def band_kernel(qid, kid, bs, *refs):
    keys, values, outs = refs[:SIDE], refs[SIDE : 2 * SIDE], refs[-3:]
    for s in range(SIDE):
        for i, out in enumerate(outs):
            first = bs[qid[i] * FRAMES + kid[s]]
            second = jnp.where(first == NB - 1, 0, first + 1)
            for j, source in enumerate((keys[s], values[s])):
                out[s, j, 0:BLOCK, :] = source[0, block_rows(first), :]
                out[s, j, BLOCK:, :] = source[0, block_rows(second), :]


def bands(qid, kid, bs, pieces, *after):
    shape = (SIDE, 2, 2 * BLOCK, HD)
    return pl.pallas_call(
        band_kernel,
        grid_spec=pltpu.PrefetchScalarGridSpec(
            num_scalar_prefetch=3,
            grid=(1,),
            in_specs=[pl.BlockSpec((1, FT, HD), lambda i, *_, j=j: (j, 0, 0)) for j in (3, 4) for _ in pieces]
            + [ANY] * len(after),
            out_specs=[pl.BlockSpec(shape, lambda i, *_: (0, 0, 0, 0))] * 3,
        ),
        out_shape=[jax.ShapeDtypeStruct(shape, jnp.bfloat16)] * 3,
        name="bands",
    )(qid, kid, bs, *pieces, *pieces, *after)


def place(n, keys, values, row, kc, vc, valid=None, stand_in=None):
    ones = lax.broadcasted_iota(jnp.int32, (BLOCK, HD), 1) == 0
    at = slice(n * BLOCK, (n + 1) * BLOCK)
    if valid is None:
        kc[at, :] = keys[block_rows(row), :]
        vc[at, 0:HD] = values[block_rows(row), :]
        vc[at, HD:] = ones.astype(jnp.bfloat16)
    else:
        kc[at, :] = keys[block_rows(jnp.where(valid, row, stand_in)), :]
        kept = jnp.where(valid, 1.0, 0.0)
        vc[at, 0:HD] = (values[block_rows(row), :].astype(jnp.float32) * kept).astype(jnp.bfloat16)
        vc[at, HD:] = jnp.where(ones, kept, 0.0).astype(jnp.bfloat16)


def band_of(a, b, bs, bw):
    own = a == b
    first = jnp.where(own, 0, bs[a * FRAMES + b])
    second = jnp.where(first == NB - 1, 0, first + 1)
    return first, second, own | (bw[jnp.abs(a - b)] == 2)


def attend_to(q, kc, vc, state, emit):
    kk, vv = kc[...], vc[...]
    steps = FT // ROWS

    def score(r):
        return lax.dot_general(q[r * ROWS : (r + 1) * ROWS, :], kk, NT, preferred_element_type=jnp.float32)

    scores = score(0)
    for r in range(steps):
        later = score(r + 1) if r + 1 < steps else None
        rows = slice(r * ROWS, (r + 1) * ROWS)
        new = jnp.max(scores, axis=1, keepdims=True)
        if state:
            old = state[1][0, rows, 0:1]
            new = jnp.maximum(old, new)
        probs = jnp.exp2(scores * LOG2_SCALE - new * LOG2_SCALE).astype(jnp.bfloat16)
        mixed = lax.dot_general(probs, vv, NN, preferred_element_type=jnp.float32)
        weighted, totals = mixed[:, 0:HD], mixed[:, HD : HD + 1]
        if state:
            factor = jnp.exp2((old - new) * LOG2_SCALE)
            weighted = weighted + state[0][0, rows, :] * factor
            totals = totals + state[1][0, rows, 1:2] * factor
        emit(rows, weighted, totals, new)
        scores = later


def put_state(acc, stats):
    def emit(rows, weighted, totals, new):
        acc[0, rows, :] = weighted
        column = lax.broadcasted_iota(jnp.int32, (ROWS, HD), 1)
        stats[0, rows, :] = jnp.where(column == 0, new, totals)

    return emit


def put_result(out):
    def emit(rows, weighted, totals, new):
        out[0, rows, :] = (weighted / totals).astype(jnp.bfloat16)

    return emit


def line_kernel(qid, kid, bs, bw, p0, p1, p2, p3, q_last, acc, stats, q, kc, vc):
    i = pl.program_id(0)
    which = jnp.where(i == SIDE, 3, 1)
    own = jnp.where(i == SIDE, 0, i)
    for s, piece in enumerate((p0, p1, p2, p3)):
        keys, values = piece.at[which], piece.at[which + 1]
        first, second, valid = band_of(qid[i], kid[s], bs, bw)
        place(2 * s, keys, values, first, kc, vc)
        place(2 * s + 1, keys, values, second, kc, vc, valid, first)

        @pl.when(own == s)
        def _(keys=keys, values=values):
            for j in range(2, NB):
                place(2 * SIDE + j - 2, keys, values, j, kc, vc)

        @pl.when(i == s)
        def _(piece=piece):
            q[...] = piece[0]

    @pl.when(i == SIDE)
    def _():
        q[...] = q_last[...]

    attend_to(q, kc, vc, None, put_state(acc, stats))


ITEM = pl.BlockSpec((1, FT, HD), lambda i, *_: (i, 0, 0))


def cost(items, blocks):
    pairs_read = items * FT * blocks * BLOCK
    return pl.CostEstimate(flops=pairs_read * 4 * HD, bytes_accessed=8 << 20, transcendentals=pairs_read)


def packed(blocks):
    return [pltpu.VMEM((blocks * BLOCK, HD), jnp.bfloat16), pltpu.VMEM((blocks * BLOCK, 2 * HD), jnp.bfloat16)]


def state_shape(items):
    return [jax.ShapeDtypeStruct((items, FT, HD), jnp.float32)] * 2


def attend_line(qid, kid, bs, bw, pieces, queries):
    blocks = 2 * SIDE + NB - 2
    items = SIDE + 1
    return pl.pallas_call(
        line_kernel,
        grid_spec=pltpu.PrefetchScalarGridSpec(
            num_scalar_prefetch=4,
            grid=(items,),
            in_specs=[pl.BlockSpec((5, FT, HD), lambda i, *_: (0, 0, 0))] * SIDE
            + [pl.BlockSpec((FT, HD), lambda i, *_: (0, SIDE))],
            out_specs=[ITEM, ITEM],
            scratch_shapes=[pltpu.VMEM((FT, HD), jnp.bfloat16)] + packed(blocks),
        ),
        out_shape=state_shape(items),
        compiler_params=pltpu.CompilerParams(vmem_limit_bytes=LIMIT),
        cost_estimate=cost(items, blocks),
        name="attend_line",
    )(qid, kid, bs, bw, *pieces, queries)


def groups_kernel(count, finished, qid, kid, bs, bw, *refs):
    q_refs, groups, refs = refs[:SIDE], refs[SIDE : SIDE + count], refs[SIDE + count :]
    state, results, (q, kc, vc) = refs[:2], refs[2:-3], refs[-3:]
    i = pl.program_id(0)
    for s, q_ref in enumerate(q_refs):

        @pl.when(i == s)
        def _(q_ref=q_ref):
            q[...] = q_ref[0]

    for d in range(count // 2):
        for s in range(SIDE):
            n = d * SIDE + s
            keys, values = groups[2 * d].at[s], groups[2 * d + 1].at[s]
            first, second, valid = band_of(qid[i], kid[n], bs, bw)
            place(2 * n, keys, values, first, kc, vc)
            place(2 * n + 1, keys, values, second, kc, vc, valid, first)
    attend_to(q, kc, vc, state, put_result(*results) if finished else put_state(*results))


def attend_groups(qid, kid, bs, bw, pieces, groups, state, finished=False):
    blocks = SIDE * len(groups)
    whole = pl.BlockSpec((SIDE, FT, HD), lambda i, *_: (0, 0, 0))
    return pl.pallas_call(
        functools.partial(groups_kernel, len(groups), finished),
        grid_spec=pltpu.PrefetchScalarGridSpec(
            num_scalar_prefetch=4,
            grid=(SIDE,),
            in_specs=[pl.BlockSpec((1, FT, HD), lambda i, *_: (0, 0, 0))] * SIDE + [whole] * len(groups) + [ITEM] * 2,
            out_specs=ITEM if finished else [ITEM] * 2,
            scratch_shapes=[pltpu.VMEM((FT, HD), jnp.bfloat16)] + packed(blocks),
        ),
        out_shape=jax.ShapeDtypeStruct((SIDE, FT, HD), jnp.bfloat16) if finished else state_shape(SIDE),
        compiler_params=pltpu.CompilerParams(vmem_limit_bytes=LIMIT),
        cost_estimate=cost(SIDE, blocks),
        name="attend_groups",
    )(qid, kid, bs, bw, *pieces, *groups, *state)


def bands_attend_kernel(qid, kid, bs, bw, q, g1, g2, g3, acc, stats, after, out, kc, vc):
    del after
    for d, group in enumerate((g1, g2, g3)):
        for s in range(SIDE):
            n = d * SIDE + s
            valid = band_of(qid[0], kid[n], bs, bw)[2]
            place(2 * n, group.at[s, 0], group.at[s, 1], 0, kc, vc)
            place(2 * n + 1, group.at[s, 0], group.at[s, 1], 1, kc, vc, valid, 0)
    attend_to(q, kc, vc, (acc, stats), put_result(out))


def attend_bands(qid, kid, bs, bw, queries, groups, state, after):
    blocks = 2 * SIDE * len(groups)
    last = pl.BlockSpec((1, FT, HD), lambda i, *_: (SIDE, 0, 0))
    return pl.pallas_call(
        bands_attend_kernel,
        grid_spec=pltpu.PrefetchScalarGridSpec(
            num_scalar_prefetch=4,
            grid=(1,),
            in_specs=[pl.BlockSpec((FT, HD), lambda i, *_: (0, SIDE))]
            + [pl.BlockSpec(g.shape, lambda i, *_: (0, 0, 0, 0)) for g in groups]
            + [last, last, ANY],
            out_specs=ITEM,
            scratch_shapes=packed(blocks),
        ),
        out_shape=jax.ShapeDtypeStruct((1, FT, HD), jnp.bfloat16),
        compiler_params=pltpu.CompilerParams(vmem_limit_bytes=LIMIT),
        cost_estimate=cost(1, blocks),
        name="attend_bands",
    )(qid, kid, bs, bw, queries, *groups, *state, after)


def project_kernel(order, pos, o0, o1, o2, o3, o4, w_ref, *refs):
    y_ref, att = refs[-2:]
    for s, o in enumerate((o0, o1, o2, o3)):
        head = lax.rem(pos[0] + s, SIDE)
        att[:, pl.ds(pl.multiple_of(head * HD, HD), HD)] = o[...]
    att[:, 4 * HD :] = o4[...]
    width = y_ref.shape[2]
    for i in range(y_ref.shape[0]):
        weight = w_ref[:, pl.ds(pl.multiple_of(order[i] * width, width), width)]
        y_ref[i] = jnp.dot(att[...], weight, preferred_element_type=jnp.float32).astype(jnp.bfloat16)


def project(order, pos, outs, weight, *after):
    count = order.shape[0]
    width = weight.shape[1] // 8
    smem = pl.BlockSpec(memory_space=pltpu.SMEM)
    return pl.pallas_call(
        project_kernel,
        in_specs=[smem] * 2 + [VMEM] * 6 + [ANY] * len(after),
        out_specs=VMEM,
        scratch_shapes=[pltpu.VMEM((FT, 5 * HD), jnp.bfloat16)],
        out_shape=jax.ShapeDtypeStruct((count, FT, width), jnp.bfloat16),
        compiler_params=pltpu.CompilerParams(vmem_limit_bytes=LIMIT),
        cost_estimate=pl.CostEstimate(
            flops=2 * count * FT * 5 * HD * width, bytes_accessed=count * FT * width * 2, transcendentals=0
        ),
        name="project",
    )(order, pos, *outs, weight, *after)


def add(*terms):
    total = terms[0].astype(jnp.float32)
    for t in terms[1:]:
        total = total + t.astype(jnp.float32)
    return total.astype(jnp.bfloat16)


def shards(queries, key_rows, value_rows, out_weight, band_start, band_width):
    frame, head = lax.axis_index("frame"), lax.axis_index("head")
    x, z = frame // SIDE, frame % SIDE
    y, core = head // 2, head % 2
    line = jnp.where(core == 0, z, x)
    ring = jnp.arange(SIDE, dtype=jnp.int32)

    def frames_at(cross, along):
        return jnp.where(
            core == 0,
            (x - cross) % SIDE * SIDE + (z - along) % SIDE,
            (x - along) % SIDE * SIDE + (z - cross) % SIDE,
        )

    f0, f1, f2, f3 = [frames_at(d, ring) for d in range(SIDE)]
    bs, bw = band_start.reshape(-1), band_width

    pieces = pick(line[None], queries, key_rows, value_rows)
    pieces = [pieces[0]] + [line_shift(pieces[s], s) for s in range(1, SIDE)]
    k_0, v_0 = jnp.stack([p[1] for p in pieces]), jnp.stack([p[2] for p in pieces])

    k_1, v_3 = cross_shift(k_0, 1), cross_shift(v_0, 3)
    v_1, k_3 = cross_shift(v_0, 1), cross_shift(k_0, 3)
    state = attend_line(f0, f0, bs, bw, pieces, queries)
    k_1, v_3 = fence((k_1, v_3), state[1])
    k_2, v_2 = cross_shift(k_1, 1), cross_shift(v_3, 3)

    sent = bands(frames_at(-ring[1:], 0), f0, bs, pieces, v_1, k_3)
    last_1, last_2, last_3 = [cross_shift(sent[s - 1], s) for s in range(1, SIDE)]

    main = attend_groups(
        f0, jnp.concatenate([f1, f3]), bs, bw, pieces, [k_1, v_1, k_3, v_3], state
    )
    o_main = attend_groups(f0, f2, bs, bw, pieces, [k_2, v_2], main, True)
    outs = [o_main[0]] + [line_shift(o_main[s], SIDE - s) for s in range(1, SIDE)]
    o_last = attend_bands(
        frame[None], jnp.concatenate([f1, f2, f3]), bs, bw, queries, [last_1, last_2, last_3], state, o_main
    )
    outs.append(o_last[0])

    def summed(ahead, *after):
        target = (y + jnp.array(ahead, jnp.int32)) % SIDE * 2
        away = project(target + 1 - core, line[None], outs, out_weight, *after)
        given = core_swap(away)
        kept = project(target + core, line[None], outs, out_weight, away)
        return [add(kept[i], given[i]) for i in range(len(ahead))]

    half = FT // 2
    (two,) = summed([2])
    from_down, from_up = y_shift(two[:half], 1), y_shift(two[half:], 3)
    up, down = summed([1, 3], two)
    plain_up, plain_down = y_shift(up[half:], 1), y_shift(down[:half], 3)
    (own,) = summed([0], up)
    more_up, more_down = y_shift(add(up[:half], from_down), 1), y_shift(add(down[half:], from_up), 3)
    return jnp.concatenate([add(own[:half], more_up, plain_down), add(own[half:], plain_up, more_down)])


def solution(mesh):
    return jax.shard_map(
        shards,
        mesh=mesh,
        in_specs=(
            P("frame", "head"),
            P("frame", "head"),
            P("frame", "head"),
            P("head", None),
            P(),
            P(),
        ),
        out_specs=P("frame", "head"),
        check_vma=False,
    )
```

```python
import functools

import jax
import jax.numpy as jnp
from jax import lax
from jax.experimental import pallas as pl
from jax.experimental.pallas import tpu as pltpu
from jax.sharding import PartitionSpec as P

HD = 128
BLOCK = 128
NB = 5
FT = 640
FRAMES = 16
SIDE = 4
ROWS = 128
LOG2_SCALE = 1.4426950408889634 / HD**0.5
NT = (((1,), (1,)), ((), ()))
NN = (((1,), (0,)), ((), ()))
BOTH = ("frame", "head")


def pairs(move):
    out = []
    for i in range(128):
        frame, head = divmod(i, 8)
        x, z, y, c = move(*divmod(frame, 4), *divmod(head, 2))
        out.append((i, (x % 4 * 4 + z % 4) * 8 + y % 4 * 2 + c))
    return out


def line_shift(v, s):
    return lax.ppermute(v, BOTH, pairs(lambda x, z, y, c: (x, z + s, y, c) if c == 0 else (x + s, z, y, c)))


def cross_shift(v, s):
    return lax.ppermute(v, BOTH, pairs(lambda x, z, y, c: (x + s, z, y, c) if c == 0 else (x, z + s, y, c)))


def y_shift(v, s):
    return lax.ppermute(v, BOTH, pairs(lambda x, z, y, c: (x, z, y + s, c)))


def core_swap(v):
    return lax.ppermute(v, BOTH, pairs(lambda x, z, y, c: (x, z, y, 1 - c)))


ANY = pl.BlockSpec(memory_space=pl.ANY)
VMEM = pl.BlockSpec(memory_space=pltpu.VMEM)
LIMIT = 20 << 20


def in_hbm(*arrays):
    return [pltpu.with_memory_space_constraint(v, pltpu.HBM) for v in arrays]


def pick_kernel(pos, q_any, k_any, v_any, *refs):
    outs, (q, k, v, sems) = refs[:SIDE], refs[SIDE:]
    rows = FT // 5
    copies = []
    for i in range(5):
        part = pl.ds(i * rows, rows)
        for j, (source, target) in enumerate(((q_any, q), (k_any, k), (v_any, v))):
            copies.append(pltpu.make_async_copy(source.at[part, :], target.at[part, :], sems.at[3 * i + j]))
    for copy in copies:
        copy.start()
    for i in range(5):
        for copy in copies[3 * i : 3 * i + 3]:
            copy.wait()
        part = slice(i * rows, (i + 1) * rows)
        for s, out in enumerate(outs):
            head = lax.rem(pos[0] + s, SIDE)
            columns = pl.ds(pl.multiple_of(head * HD, HD), HD)
            out[0, part, :] = q[part, columns]
            out[1, part, :] = k[part, columns]
            out[2, part, :] = v[part, columns]
            out[3, part, :] = k[part, 4 * HD :]
            out[4, part, :] = v[part, 4 * HD :]


def pick(pos, queries, keys, values):
    return pl.pallas_call(
        pick_kernel,
        in_specs=[pl.BlockSpec(memory_space=pltpu.SMEM)] + [ANY] * 3,
        out_specs=[VMEM] * SIDE,
        out_shape=[pltpu.VMEM((5, FT, HD), jnp.bfloat16)] * SIDE,
        scratch_shapes=[pltpu.VMEM((FT, 5 * HD), jnp.bfloat16)] * 3 + [pltpu.SemaphoreType.DMA((15,))],
        compiler_params=pltpu.CompilerParams(vmem_limit_bytes=LIMIT),
        name="pick",
    )(pos, *in_hbm(queries, keys, values))


def stack_kernel(*refs):
    pieces, (q, kv, k_last, v_last, sems) = refs[:SIDE], refs[SIDE:]
    copies = []
    for s, piece in enumerate(pieces):
        targets = (q.at[s], kv.at[s], kv.at[SIDE + s], k_last.at[s], v_last.at[s])
        for j, target in enumerate(targets):
            copies.append(pltpu.make_async_copy(piece.at[j], target, sems.at[s, j]))
    for copy in copies:
        copy.start()
    for copy in copies:
        copy.wait()


def stack(pieces):
    shape = (SIDE, FT, HD)
    both = (2 * SIDE, FT, HD)
    return pl.pallas_call(
        stack_kernel,
        in_specs=[VMEM] * SIDE,
        out_specs=[ANY] * 4,
        out_shape=[pltpu.HBM(s, jnp.bfloat16) for s in (shape, both, shape, shape)],
        scratch_shapes=[pltpu.SemaphoreType.DMA((SIDE, 5))],
        compiler_params=pltpu.CompilerParams(vmem_limit_bytes=LIMIT),
        name="stack",
    )(*pieces)


def block_rows(n):
    return pl.ds(pl.multiple_of(n * BLOCK, BLOCK), BLOCK)


def place(n, keys, values, row, kc, vc, valid=None, stand_in=None):
    ones = lax.broadcasted_iota(jnp.int32, (BLOCK, HD), 1) == 0
    at = slice(n * BLOCK, (n + 1) * BLOCK)
    if valid is None:
        kc[at, :] = keys[block_rows(row), :]
        vc[at, 0:HD] = values[block_rows(row), :]
        vc[at, HD:] = ones.astype(jnp.bfloat16)
    else:
        kc[at, :] = keys[block_rows(jnp.where(valid, row, stand_in)), :]
        taken = values[block_rows(row), :]
        vc[at, 0:HD] = jnp.where(valid, taken, jnp.zeros_like(taken))
        vc[at, HD:] = jnp.where(ones & valid, 1.0, 0.0).astype(jnp.bfloat16)


def band_of(a, b, bs, bw):
    own = a == b
    first = jnp.where(own, 0, bs[a * FRAMES + b])
    second = jnp.where(first == NB - 1, 0, first + 1)
    return first, second, own | (bw[jnp.abs(a - b)] == 2)


def attend_to(q, kc, vc, state, emit):
    kk, vv = kc[...], vc[...]
    steps = FT // ROWS

    def score(r):
        return lax.dot_general(q[r * ROWS : (r + 1) * ROWS, :], kk, NT, preferred_element_type=jnp.float32)

    scores = score(0)
    for r in range(steps):
        later = score(r + 1) if r + 1 < steps else None
        rows = slice(r * ROWS, (r + 1) * ROWS)
        top = jnp.max(scores, axis=1, keepdims=True) * LOG2_SCALE
        if state:
            level = jnp.broadcast_to(state[1][0, r : r + 1, :], (ROWS, HD)).T[:, 0:1]
            top = jnp.maximum(top, level)
        probs = jnp.exp2(scores * LOG2_SCALE - top).astype(jnp.bfloat16)
        mixed = lax.dot_general(probs, vv, NN, preferred_element_type=jnp.float32)
        weighted, totals = mixed[:, 0:HD], mixed[:, HD : HD + 1]
        if state:
            share = jnp.exp2(level - top)
            weighted = weighted + state[0][0, rows, :].astype(jnp.float32) * share
            totals = totals + share
        emit(r, (weighted / totals).astype(jnp.bfloat16), top, totals)
        scores = later


def put_state(out, levels):
    def emit(r, result, top, totals):
        out[0, r * ROWS : (r + 1) * ROWS, :] = result
        level = top + jnp.log2(totals)
        levels[0, r : r + 1, :] = jnp.broadcast_to(level, (ROWS, HD)).T[0:1, :]

    return emit


def put_result(out):
    def emit(r, result, top, totals):
        out[0, r * ROWS : (r + 1) * ROWS, :] = result

    return emit


def line_kernel(qid, kid, bs, bw, q, kv, out, levels, kc, vc):
    i = pl.program_id(0)
    for s in range(SIDE):
        first, second, valid = band_of(qid[i], kid[s], bs, bw)
        place(2 * s, kv.at[s], kv.at[SIDE + s], first, kc, vc)
        place(2 * s + 1, kv.at[s], kv.at[SIDE + s], second, kc, vc, valid, first)
    for j in range(2, NB):
        place(2 * SIDE + j - 2, kv.at[i], kv.at[SIDE + i], j, kc, vc)
    attend_to(q.at[0], kc, vc, None, put_state(out, levels))


def last_line_kernel(qid, kid, bs, bw, q, keys, values, after, out, levels, s1, s2, s3, kc, vc):
    del after
    for s in range(SIDE):
        for i, sent in enumerate((s1, s2, s3)):
            first, second, unused = band_of(qid[i + 1], kid[s], bs, bw)
            for j, source in enumerate((keys, values)):
                sent[s, j, 0:BLOCK, :] = source[s, block_rows(first), :]
                sent[s, j, BLOCK:, :] = source[s, block_rows(second), :]
    for j in range(NB):
        place(j, keys.at[0], values.at[0], j, kc, vc)
    for s in range(1, SIDE):
        first, second, valid = band_of(qid[0], kid[s], bs, bw)
        n = NB + 2 * (s - 1)
        place(n, keys.at[s], values.at[s], first, kc, vc)
        place(n + 1, keys.at[s], values.at[s], second, kc, vc, valid, first)
    attend_to(q, kc, vc, None, put_state(out, levels))


ITEM = pl.BlockSpec((1, FT, HD), lambda i, *_: (i, 0, 0))
LEVEL = pl.BlockSpec((1, 8, HD), lambda i, *_: (i, 0, 0))


def cost(items, blocks):
    pairs_read = items * FT * blocks * BLOCK
    return pl.CostEstimate(flops=pairs_read * 4 * HD, bytes_accessed=8 << 20, transcendentals=pairs_read)


def packed(blocks):
    return [pltpu.VMEM((blocks * BLOCK, HD), jnp.bfloat16), pltpu.VMEM((blocks * BLOCK, 2 * HD), jnp.bfloat16)]


def state_shape(items):
    return [pltpu.HBM((items, FT, HD), jnp.bfloat16), pltpu.HBM((items, 8, HD), jnp.float32)]


def attend_line(qid, kid, bs, bw, q, kv):
    blocks = 2 * SIDE + NB - 2
    return pl.pallas_call(
        line_kernel,
        grid_spec=pltpu.PrefetchScalarGridSpec(
            num_scalar_prefetch=4,
            grid=(SIDE,),
            in_specs=[ITEM, pl.BlockSpec(kv.shape, lambda i, *_: (0, 0, 0))],
            out_specs=[ITEM, LEVEL],
            scratch_shapes=packed(blocks),
        ),
        out_shape=state_shape(SIDE),
        compiler_params=pltpu.CompilerParams(vmem_limit_bytes=LIMIT),
        cost_estimate=cost(SIDE, blocks),
        name="attend_line",
    )(qid, kid, bs, bw, *in_hbm(q, kv))


def attend_last_line(qid, kid, bs, bw, queries, keys, values, after):
    blocks = 2 * SIDE + NB - 2
    whole = pl.BlockSpec((SIDE, FT, HD), lambda i, *_: (0, 0, 0))
    sent = (SIDE, 2, 2 * BLOCK, HD)
    return pl.pallas_call(
        last_line_kernel,
        grid_spec=pltpu.PrefetchScalarGridSpec(
            num_scalar_prefetch=4,
            grid=(1,),
            in_specs=[pl.BlockSpec((FT, HD), lambda i, *_: (0, SIDE)), whole, whole, ANY],
            out_specs=[ITEM, LEVEL] + [pl.BlockSpec(sent, lambda i, *_: (0, 0, 0, 0))] * 3,
            scratch_shapes=packed(blocks),
        ),
        out_shape=state_shape(1) + [pltpu.HBM(sent, jnp.bfloat16)] * 3,
        compiler_params=pltpu.CompilerParams(vmem_limit_bytes=LIMIT),
        cost_estimate=cost(1, blocks),
        name="attend_last_line",
    )(qid, kid, bs, bw, *in_hbm(queries, keys, values, after))


def groups_kernel(count, finished, qid, kid, bs, bw, q, *refs):
    groups, (before, levels), results, (kc, vc) = refs[:count], refs[count : count + 2], refs[count + 2 : -2], refs[-2:]
    i = pl.program_id(0)
    for d, group in enumerate(groups):
        for s in range(SIDE):
            n = d * SIDE + s
            keys, values = group.at[s], group.at[SIDE + s]
            first, second, valid = band_of(qid[i], kid[n], bs, bw)
            place(2 * n, keys, values, first, kc, vc)
            place(2 * n + 1, keys, values, second, kc, vc, valid, first)
    if finished:
        out, token = results
        token[...] = jnp.zeros(token.shape, token.dtype)
        emit = put_result(out)
    else:
        emit = put_state(*results)
    attend_to(q.at[0], kc, vc, (before, levels), emit)


def attend_groups(qid, kid, bs, bw, q, groups, state, finished):
    blocks = 2 * SIDE * len(groups)
    if finished:
        out_specs = [ITEM, pl.BlockSpec((8, HD), lambda i, *_: (0, 0))]
        out_shape = [jax.ShapeDtypeStruct((SIDE, FT, HD), jnp.bfloat16), pltpu.HBM((8, HD), jnp.float32)]
    else:
        out_specs, out_shape = [ITEM, LEVEL], state_shape(SIDE)
    return pl.pallas_call(
        functools.partial(groups_kernel, len(groups), finished),
        grid_spec=pltpu.PrefetchScalarGridSpec(
            num_scalar_prefetch=4,
            grid=(SIDE,),
            in_specs=[ITEM] + [pl.BlockSpec(g.shape, lambda i, *_: (0, 0, 0)) for g in groups] + [ITEM, LEVEL],
            out_specs=out_specs,
            scratch_shapes=packed(blocks),
        ),
        out_shape=out_shape,
        compiler_params=pltpu.CompilerParams(vmem_limit_bytes=LIMIT),
        cost_estimate=cost(SIDE, blocks),
        name="attend_groups",
    )(qid, kid, bs, bw, *in_hbm(q), *groups, *in_hbm(*state))


def bands_attend_kernel(qid, kid, bs, bw, q, g1, g2, g3, before, levels, after, out, kc, vc):
    del after
    for d, group in enumerate((g1, g2, g3)):
        for s in range(SIDE):
            n = d * SIDE + s
            valid = band_of(qid[0], kid[n], bs, bw)[2]
            place(2 * n, group.at[s, 0], group.at[s, 1], 0, kc, vc)
            place(2 * n + 1, group.at[s, 0], group.at[s, 1], 1, kc, vc, valid, 0)
    attend_to(q, kc, vc, (before, levels), put_result(out))


def attend_bands(qid, kid, bs, bw, queries, groups, state, after):
    blocks = 2 * SIDE * len(groups)
    return pl.pallas_call(
        bands_attend_kernel,
        grid_spec=pltpu.PrefetchScalarGridSpec(
            num_scalar_prefetch=4,
            grid=(1,),
            in_specs=[pl.BlockSpec((FT, HD), lambda i, *_: (0, SIDE))]
            + [pl.BlockSpec(g.shape, lambda i, *_: (0, 0, 0, 0)) for g in groups]
            + [ITEM, LEVEL, ANY],
            out_specs=ITEM,
            scratch_shapes=packed(blocks),
        ),
        out_shape=jax.ShapeDtypeStruct((1, FT, HD), jnp.bfloat16),
        compiler_params=pltpu.CompilerParams(vmem_limit_bytes=LIMIT),
        cost_estimate=cost(1, blocks),
        name="attend_bands",
    )(qid, kid, bs, bw, *in_hbm(queries), *groups, *in_hbm(*state, after))


def project_kernel(order, pos, o0, o1, o2, o3, o4, w_ref, *refs):
    y_ref, att = refs[-2:]

    @pl.when(pl.program_id(0) == 0)
    def _():
        for s, o in enumerate((o0, o1, o2, o3)):
            head = lax.rem(pos[0] + s, SIDE)
            att[:, pl.ds(pl.multiple_of(head * HD, HD), HD)] = o[...]
        att[:, 4 * HD :] = o4[...]

    y_ref[0] = jnp.dot(att[...], w_ref[...], preferred_element_type=jnp.float32).astype(jnp.bfloat16)


def project(order, pos, outs, weight, *after):
    count = order.shape[0]
    width = weight.shape[1] // 8
    whole = pl.BlockSpec((FT, HD), lambda i, *_: (0, 0))
    return pl.pallas_call(
        project_kernel,
        grid_spec=pltpu.PrefetchScalarGridSpec(
            num_scalar_prefetch=2,
            grid=(count,),
            in_specs=[whole] * 5
            + [pl.BlockSpec((5 * HD, width), lambda i, order, pos: (0, order[i]))]
            + [ANY] * len(after),
            out_specs=pl.BlockSpec((1, FT, width), lambda i, *_: (i, 0, 0)),
            scratch_shapes=[pltpu.VMEM((FT, 5 * HD), jnp.bfloat16)],
        ),
        out_shape=jax.ShapeDtypeStruct((count, FT, width), jnp.bfloat16),
        compiler_params=pltpu.CompilerParams(vmem_limit_bytes=LIMIT),
        cost_estimate=pl.CostEstimate(
            flops=2 * count * FT * 5 * HD * width, bytes_accessed=count * FT * width * 2, transcendentals=0
        ),
        name="project",
    )(order, pos, *outs, *in_hbm(weight), *after)


def add(*terms):
    total = terms[0].astype(jnp.float32)
    for t in terms[1:]:
        total = total + t.astype(jnp.float32)
    return total.astype(jnp.bfloat16)


def finish_kernel(own, more_up, plain_up, more_down, plain_down, out):
    half = FT // 2
    wide = lambda v: v.astype(jnp.float32)
    out[0:half, :] = (wide(own[0:half, :]) + wide(more_up[...]) + wide(plain_down[...])).astype(jnp.bfloat16)
    out[half:, :] = (wide(own[half:, :]) + wide(more_down[...]) + wide(plain_up[...])).astype(jnp.bfloat16)


def finish(*args):
    return pl.pallas_call(
        finish_kernel,
        in_specs=[VMEM] * 5,
        out_specs=pl.BlockSpec(args[0].shape, lambda: (0, 0)),
        out_shape=jax.ShapeDtypeStruct(args[0].shape, jnp.bfloat16),
        compiler_params=pltpu.CompilerParams(vmem_limit_bytes=LIMIT),
        name="finish",
    )(*args)


def shards(queries, key_rows, value_rows, out_weight, band_start, band_width):
    frame, head = lax.axis_index("frame"), lax.axis_index("head")
    x, z = frame // SIDE, frame % SIDE
    y, core = head // 2, head % 2
    line = jnp.where(core == 0, z, x)
    ring = jnp.arange(SIDE, dtype=jnp.int32)

    def frames_at(cross, along):
        return jnp.where(
            core == 0,
            (x - cross) % SIDE * SIDE + (z - along) % SIDE,
            (x - along) % SIDE * SIDE + (z - cross) % SIDE,
        )

    f0, f1, f2, f3 = [frames_at(d, ring) for d in range(SIDE)]
    bs, bw = band_start.reshape(-1), band_width

    pieces = pick(line[None], queries, key_rows, value_rows)
    pieces = [pieces[0]] + [line_shift(pieces[s], s) for s in range(1, SIDE)]
    q, kv, k_last, v_last = stack(pieces)

    groups = [cross_shift(kv, s) for s in range(1, SIDE)]
    state = attend_line(f0, f0, bs, bw, q, kv)

    here_and_across = frames_at(-ring, 0)
    *last_state, s_1, s_2, s_3 = attend_last_line(here_and_across, f0, bs, bw, queries, k_last, v_last, state[0])
    last = [cross_shift(sent, s) for s, sent in ((1, s_1), (2, s_2), (3, s_3))]

    state = attend_groups(f0, f1, bs, bw, q, groups[:1], state, False)
    o_main, token = attend_groups(f0, jnp.concatenate([f2, f3]), bs, bw, q, groups[1:], state, True)
    outs = [o_main[0]] + [line_shift(o_main[s], SIDE - s) for s in range(1, SIDE)]
    o_last = attend_bands(frame[None], jnp.concatenate([f1, f2, f3]), bs, bw, queries, last, last_state, token)
    outs.append(o_last[0])

    def summed(ahead, *after):
        target = (y + jnp.array(ahead, jnp.int32)) % SIDE * 2
        away = project(target + 1 - core, line[None], outs, out_weight, *after)
        given = core_swap(away)
        kept = project(target + core, line[None], outs, out_weight, away)
        return [add(kept[i], given[i]) for i in range(len(ahead))]

    half = FT // 2
    (two,) = summed([2])
    from_down, from_up = y_shift(two[:half], 1), y_shift(two[half:], 3)
    up, down = summed([1, 3], two)
    plain_up, plain_down = y_shift(up[half:], 1), y_shift(down[:half], 3)
    (own,) = summed([0], up)
    more_up, more_down = y_shift(add(up[:half], from_down), 1), y_shift(add(down[half:], from_up), 3)
    return finish(own, more_up, plain_up, more_down, plain_down)


def solution(mesh):
    return jax.shard_map(
        shards,
        mesh=mesh,
        in_specs=(
            P("frame", "head"),
            P("frame", "head"),
            P("frame", "head"),
            P("head", None),
            P(),
            P(),
        ),
        out_specs=P("frame", "head"),
        check_vma=False,
    )
```

```python
import functools

import jax
import jax.numpy as jnp
from jax import lax
from jax.experimental import pallas as pl
from jax.experimental.pallas import tpu as pltpu
from jax.sharding import PartitionSpec as P

HD = 128
BLOCK = 128
NB = 5
FT = 640
FRAMES = 16
SIDE = 4
ROWS = 128
LOG2_SCALE = 1.4426950408889634 / HD**0.5
NT = (((1,), (1,)), ((), ()))
NN = (((1,), (0,)), ((), ()))
BOTH = ("frame", "head")


def pairs(move):
    out = []
    for i in range(128):
        frame, head = divmod(i, 8)
        x, z, y, c = move(*divmod(frame, 4), *divmod(head, 2))
        out.append((i, (x % 4 * 4 + z % 4) * 8 + y % 4 * 2 + c))
    return out


def line_shift(v, s):
    return lax.ppermute(v, BOTH, pairs(lambda x, z, y, c: (x, z + s, y, c) if c == 0 else (x + s, z, y, c)))


def cross_shift(v, s):
    return lax.ppermute(v, BOTH, pairs(lambda x, z, y, c: (x + s, z, y, c) if c == 0 else (x, z + s, y, c)))


def y_shift(v, s):
    return lax.ppermute(v, BOTH, pairs(lambda x, z, y, c: (x, z, y + s, c)))


def core_swap(v):
    return lax.ppermute(v, BOTH, pairs(lambda x, z, y, c: (x, z, y, 1 - c)))


ANY = pl.BlockSpec(memory_space=pl.ANY)
VMEM = pl.BlockSpec(memory_space=pltpu.VMEM)
LIMIT = 20 << 20


def in_hbm(*arrays):
    return [pltpu.with_memory_space_constraint(v, pltpu.HBM) for v in arrays]


def pick_kernel(pos, q_any, k_any, v_any, *refs):
    outs, (q, k, v, sems) = refs[:SIDE], refs[SIDE:]
    rows = FT // 5
    copies = []
    for i in range(5):
        part = pl.ds(i * rows, rows)
        for j, (source, target) in enumerate(((q_any, q), (k_any, k), (v_any, v))):
            copies.append(pltpu.make_async_copy(source.at[part, :], target.at[part, :], sems.at[3 * i + j]))
    for copy in copies:
        copy.start()
    for i in range(5):
        for copy in copies[3 * i : 3 * i + 3]:
            copy.wait()
        part = slice(i * rows, (i + 1) * rows)
        for s, out in enumerate(outs):
            head = lax.rem(pos[0] + s, SIDE)
            columns = pl.ds(pl.multiple_of(head * HD, HD), HD)
            out[0, part, :] = q[part, columns]
            out[1, part, :] = k[part, columns]
            out[2, part, :] = v[part, columns]
            out[3, part, :] = k[part, 4 * HD :]
            out[4, part, :] = v[part, 4 * HD :]


def pick(pos, queries, keys, values):
    return pl.pallas_call(
        pick_kernel,
        in_specs=[pl.BlockSpec(memory_space=pltpu.SMEM)] + [ANY] * 3,
        out_specs=[VMEM] * SIDE,
        out_shape=[pltpu.VMEM((5, FT, HD), jnp.bfloat16)] * SIDE,
        scratch_shapes=[pltpu.VMEM((FT, 5 * HD), jnp.bfloat16)] * 3 + [pltpu.SemaphoreType.DMA((15,))],
        compiler_params=pltpu.CompilerParams(vmem_limit_bytes=LIMIT),
        name="pick",
    )(pos, *in_hbm(queries, keys, values))


def stack_kernel(*refs):
    pieces, (q, kv, k_last, v_last, sems) = refs[:SIDE], refs[SIDE:]
    copies = []
    for s, piece in enumerate(pieces):
        targets = (q.at[s], kv.at[s], kv.at[SIDE + s], k_last.at[s], v_last.at[s])
        for j, target in enumerate(targets):
            copies.append(pltpu.make_async_copy(piece.at[j], target, sems.at[s, j]))
    for copy in copies:
        copy.start()
    for copy in copies:
        copy.wait()


def stack(pieces):
    shape = (SIDE, FT, HD)
    both = (2 * SIDE, FT, HD)
    return pl.pallas_call(
        stack_kernel,
        in_specs=[VMEM] * SIDE,
        out_specs=[ANY] * 4,
        out_shape=[pltpu.HBM(s, jnp.bfloat16) for s in (shape, both, shape, shape)],
        scratch_shapes=[pltpu.SemaphoreType.DMA((SIDE, 5))],
        compiler_params=pltpu.CompilerParams(vmem_limit_bytes=LIMIT),
        name="stack",
    )(*pieces)


def block_rows(n):
    return pl.ds(pl.multiple_of(n * BLOCK, BLOCK), BLOCK)


def place(n, keys, values, row, kc, vc, valid=None, stand_in=None):
    ones = lax.broadcasted_iota(jnp.int32, (BLOCK, HD), 1) == 0
    at = slice(n * BLOCK, (n + 1) * BLOCK)
    if valid is None:
        kc[at, :] = keys[block_rows(row), :]
        vc[at, 0:HD] = values[block_rows(row), :]
        vc[at, HD:] = ones.astype(jnp.bfloat16)
    else:
        kc[at, :] = keys[block_rows(jnp.where(valid, row, stand_in)), :]
        taken = values[block_rows(row), :]
        vc[at, 0:HD] = jnp.where(valid, taken, jnp.zeros_like(taken))
        vc[at, HD:] = jnp.where(ones & valid, 1.0, 0.0).astype(jnp.bfloat16)


def band_of(a, b, bs, bw):
    own = a == b
    first = jnp.where(own, 0, bs[a * FRAMES + b])
    second = jnp.where(first == NB - 1, 0, first + 1)
    return first, second, own | (bw[jnp.abs(a - b)] == 2)


def attend_to(q, kc, vc, state, emit):
    kk, vv = kc[...], vc[...]
    steps = FT // ROWS

    def score(r):
        return lax.dot_general(q[r * ROWS : (r + 1) * ROWS, :], kk, NT, preferred_element_type=jnp.float32)

    scores = score(0)
    for r in range(steps):
        later = score(r + 1) if r + 1 < steps else None
        rows = slice(r * ROWS, (r + 1) * ROWS)
        top = jnp.max(scores, axis=1, keepdims=True) * LOG2_SCALE
        if state:
            level = jnp.broadcast_to(state[1][0, r : r + 1, :], (ROWS, HD)).T[:, 0:1]
            top = jnp.maximum(top, level)
        probs = jnp.exp2(scores * LOG2_SCALE - top).astype(jnp.bfloat16)
        mixed = lax.dot_general(probs, vv, NN, preferred_element_type=jnp.float32)
        weighted, totals = mixed[:, 0:HD], mixed[:, HD : HD + 1]
        if state:
            share = jnp.exp2(level - top)
            weighted = weighted + state[0][0, rows, :].astype(jnp.float32) * share
            totals = totals + share
        emit(r, (weighted / totals).astype(jnp.bfloat16), top, totals)
        scores = later


def put_state(out, levels):
    def emit(r, result, top, totals):
        out[0, r * ROWS : (r + 1) * ROWS, :] = result
        level = top + jnp.log2(totals)
        levels[0, r : r + 1, :] = jnp.broadcast_to(level, (ROWS, HD)).T[0:1, :]

    return emit


def put_result(out):
    def emit(r, result, top, totals):
        out[0, r * ROWS : (r + 1) * ROWS, :] = result

    return emit


def line_kernel(qid, kid, bs, bw, q, kv, after, out, levels, kc, vc):
    del after
    i = pl.program_id(0)
    for s in range(SIDE):
        first, second, valid = band_of(qid[i], kid[s], bs, bw)
        place(2 * s, kv.at[s], kv.at[SIDE + s], first, kc, vc)
        place(2 * s + 1, kv.at[s], kv.at[SIDE + s], second, kc, vc, valid, first)
    for j in range(2, NB):
        place(2 * SIDE + j - 2, kv.at[i], kv.at[SIDE + i], j, kc, vc)
    attend_to(q.at[0], kc, vc, None, put_state(out, levels))


def last_line_kernel(qid, kid, bs, bw, q, keys, values, after, out, levels, s1, s2, s3, kc, vc):
    del after
    for s in range(SIDE):
        for i, sent in enumerate((s1, s2, s3)):
            first, second, unused = band_of(qid[i + 1], kid[s], bs, bw)
            for j, source in enumerate((keys, values)):
                sent[s, j, 0:BLOCK, :] = source[s, block_rows(first), :]
                sent[s, j, BLOCK:, :] = source[s, block_rows(second), :]
    for j in range(NB):
        place(j, keys.at[0], values.at[0], j, kc, vc)
    for s in range(1, SIDE):
        first, second, valid = band_of(qid[0], kid[s], bs, bw)
        n = NB + 2 * (s - 1)
        place(n, keys.at[s], values.at[s], first, kc, vc)
        place(n + 1, keys.at[s], values.at[s], second, kc, vc, valid, first)
    attend_to(q, kc, vc, None, put_state(out, levels))


ITEM = pl.BlockSpec((1, FT, HD), lambda i, *_: (i, 0, 0))
LEVEL = pl.BlockSpec((1, 8, HD), lambda i, *_: (i, 0, 0))


def cost(items, blocks):
    pairs_read = items * FT * blocks * BLOCK
    return pl.CostEstimate(flops=pairs_read * 4 * HD, bytes_accessed=8 << 20, transcendentals=pairs_read)


def packed(blocks):
    return [pltpu.VMEM((blocks * BLOCK, HD), jnp.bfloat16), pltpu.VMEM((blocks * BLOCK, 2 * HD), jnp.bfloat16)]


def state_shape(items):
    return [pltpu.HBM((items, FT, HD), jnp.bfloat16), pltpu.HBM((items, 8, HD), jnp.float32)]


def attend_line(qid, kid, bs, bw, q, kv, after):
    blocks = 2 * SIDE + NB - 2
    return pl.pallas_call(
        line_kernel,
        grid_spec=pltpu.PrefetchScalarGridSpec(
            num_scalar_prefetch=4,
            grid=(SIDE,),
            in_specs=[ITEM, pl.BlockSpec(kv.shape, lambda i, *_: (0, 0, 0)), ANY],
            out_specs=[ITEM, LEVEL],
            scratch_shapes=packed(blocks),
        ),
        out_shape=state_shape(SIDE),
        compiler_params=pltpu.CompilerParams(vmem_limit_bytes=LIMIT),
        cost_estimate=cost(SIDE, blocks),
        name="attend_line",
    )(qid, kid, bs, bw, *in_hbm(q, kv, after))


def attend_last_line(qid, kid, bs, bw, queries, keys, values, after):
    blocks = 2 * SIDE + NB - 2
    whole = pl.BlockSpec((SIDE, FT, HD), lambda i, *_: (0, 0, 0))
    sent = (SIDE, 2, 2 * BLOCK, HD)
    return pl.pallas_call(
        last_line_kernel,
        grid_spec=pltpu.PrefetchScalarGridSpec(
            num_scalar_prefetch=4,
            grid=(1,),
            in_specs=[pl.BlockSpec((FT, HD), lambda i, *_: (0, SIDE)), whole, whole, ANY],
            out_specs=[ITEM, LEVEL] + [pl.BlockSpec(sent, lambda i, *_: (0, 0, 0, 0))] * 3,
            scratch_shapes=packed(blocks),
        ),
        out_shape=state_shape(1) + [pltpu.HBM(sent, jnp.bfloat16)] * 3,
        compiler_params=pltpu.CompilerParams(vmem_limit_bytes=LIMIT),
        cost_estimate=cost(1, blocks),
        name="attend_last_line",
    )(qid, kid, bs, bw, *in_hbm(queries, keys, values, after))


def groups_kernel(count, finished, qid, kid, bs, bw, q, *refs):
    groups, (before, levels), results, (kc, vc) = refs[:count], refs[count : count + 2], refs[count + 2 : -2], refs[-2:]
    i = pl.program_id(0)
    for d, group in enumerate(groups):
        for s in range(SIDE):
            n = d * SIDE + s
            keys, values = group.at[s], group.at[SIDE + s]
            first, second, valid = band_of(qid[i], kid[n], bs, bw)
            place(2 * n, keys, values, first, kc, vc)
            place(2 * n + 1, keys, values, second, kc, vc, valid, first)
    if finished:
        out, token = results
        token[...] = jnp.zeros(token.shape, token.dtype)
        emit = put_result(out)
    else:
        emit = put_state(*results)
    attend_to(q.at[0], kc, vc, (before, levels), emit)


def attend_groups(qid, kid, bs, bw, q, groups, state, finished):
    blocks = 2 * SIDE * len(groups)
    if finished:
        out_specs = [ITEM, pl.BlockSpec((8, HD), lambda i, *_: (0, 0))]
        out_shape = [jax.ShapeDtypeStruct((SIDE, FT, HD), jnp.bfloat16), pltpu.HBM((8, HD), jnp.float32)]
    else:
        out_specs, out_shape = [ITEM, LEVEL], state_shape(SIDE)
    return pl.pallas_call(
        functools.partial(groups_kernel, len(groups), finished),
        grid_spec=pltpu.PrefetchScalarGridSpec(
            num_scalar_prefetch=4,
            grid=(SIDE,),
            in_specs=[ITEM] + [pl.BlockSpec(g.shape, lambda i, *_: (0, 0, 0)) for g in groups] + [ITEM, LEVEL],
            out_specs=out_specs,
            scratch_shapes=packed(blocks),
        ),
        out_shape=out_shape,
        compiler_params=pltpu.CompilerParams(vmem_limit_bytes=LIMIT),
        cost_estimate=cost(SIDE, blocks),
        name="attend_groups",
    )(qid, kid, bs, bw, *in_hbm(q), *groups, *in_hbm(*state))


def bands_attend_kernel(qid, kid, bs, bw, q, g1, g2, g3, before, levels, after, out, kc, vc):
    del after
    for d, group in enumerate((g1, g2, g3)):
        for s in range(SIDE):
            n = d * SIDE + s
            valid = band_of(qid[0], kid[n], bs, bw)[2]
            place(2 * n, group.at[s, 0], group.at[s, 1], 0, kc, vc)
            place(2 * n + 1, group.at[s, 0], group.at[s, 1], 1, kc, vc, valid, 0)
    attend_to(q, kc, vc, (before, levels), put_result(out))


def attend_bands(qid, kid, bs, bw, queries, groups, state, after):
    blocks = 2 * SIDE * len(groups)
    return pl.pallas_call(
        bands_attend_kernel,
        grid_spec=pltpu.PrefetchScalarGridSpec(
            num_scalar_prefetch=4,
            grid=(1,),
            in_specs=[pl.BlockSpec((FT, HD), lambda i, *_: (0, SIDE))]
            + [pl.BlockSpec(g.shape, lambda i, *_: (0, 0, 0, 0)) for g in groups]
            + [ITEM, LEVEL, ANY],
            out_specs=ITEM,
            scratch_shapes=packed(blocks),
        ),
        out_shape=jax.ShapeDtypeStruct((1, FT, HD), jnp.bfloat16),
        compiler_params=pltpu.CompilerParams(vmem_limit_bytes=LIMIT),
        cost_estimate=cost(1, blocks),
        name="attend_bands",
    )(qid, kid, bs, bw, *in_hbm(queries), *groups, *in_hbm(*state, after))


def assemble_kernel(pos, o0, o1, o2, o3, o4, att):
    for s, o in enumerate((o0, o1, o2, o3)):
        head = lax.rem(pos[0] + s, SIDE)
        att[:, pl.ds(pl.multiple_of(head * HD, HD), HD)] = o[...]
    att[:, SIDE * HD :] = o4[...]


def assemble(pos, outs):
    return pl.pallas_call(
        assemble_kernel,
        in_specs=[pl.BlockSpec(memory_space=pltpu.SMEM)] + [VMEM] * 5,
        out_specs=VMEM,
        out_shape=jax.ShapeDtypeStruct((FT, 5 * HD), jnp.bfloat16),
        compiler_params=pltpu.CompilerParams(vmem_limit_bytes=LIMIT),
        name="assemble",
    )(pos, *outs)


def project_kernel(order, blocks, att, att_other, w_mine, w_other, *refs):
    del order, blocks
    out, step = refs[-1], FT // 2
    for r in range(0, FT, step):
        rows = slice(r, r + step)
        total = jnp.dot(att[rows, :], w_mine[...], preferred_element_type=jnp.float32)
        total = total + jnp.dot(att_other[rows, :], w_other[...], preferred_element_type=jnp.float32)
        out[pl.program_id(0), rows, :] = total.astype(jnp.bfloat16)


def project(order, core, att, att_other, weight, other_weight, *after):
    count, width = order.shape[0], weight.shape[1] // 8
    return pl.pallas_call(
        project_kernel,
        grid_spec=pltpu.PrefetchScalarGridSpec(
            num_scalar_prefetch=2,
            grid=(count,),
            in_specs=[
                VMEM,
                VMEM,
                pl.BlockSpec((5 * HD, width), lambda i, order, blocks: (0, blocks[i])),
                pl.BlockSpec((5 * HD, width), lambda i, order, blocks: (0, blocks[i])),
            ]
            + [ANY] * len(after),
            out_specs=VMEM,
        ),
        out_shape=jax.ShapeDtypeStruct((count, FT, width), jnp.bfloat16),
        compiler_params=pltpu.CompilerParams(vmem_limit_bytes=LIMIT),
        name="project",
    )(order, 2 * order + core, att, att_other, *in_hbm(weight, other_weight), *after)


def add(*terms):
    total = terms[0].astype(jnp.float32)
    for t in terms[1:]:
        total = total + t.astype(jnp.float32)
    return total.astype(jnp.bfloat16)


def onward_kernel(near, from_down, from_up, send_up, send_down):
    half = FT // 2
    wide = lambda v: v.astype(jnp.float32)
    send_up[0:half, :] = (wide(near[0, 0:half, :]) + wide(from_down[...])).astype(jnp.bfloat16)
    send_up[half:, :] = near[0, half:, :]
    send_down[0:half, :] = near[1, 0:half, :]
    send_down[half:, :] = (wide(near[1, half:, :]) + wide(from_up[...])).astype(jnp.bfloat16)


def onward(near, from_down, from_up):
    return pl.pallas_call(
        onward_kernel,
        in_specs=[VMEM] * 3,
        out_specs=[VMEM] * 2,
        out_shape=[jax.ShapeDtypeStruct(near.shape[1:], jnp.bfloat16)] * 2,
        compiler_params=pltpu.CompilerParams(vmem_limit_bytes=LIMIT),
        name="onward",
    )(near, from_down, from_up)


def shards(queries, key_rows, value_rows, out_weight, band_start, band_width):
    frame, head = lax.axis_index("frame"), lax.axis_index("head")
    x, z = frame // SIDE, frame % SIDE
    y, core = head // 2, head % 2
    line = jnp.where(core == 0, z, x)
    ring = jnp.arange(SIDE, dtype=jnp.int32)

    def frames_at(cross, along):
        return jnp.where(
            core == 0,
            (x - cross) % SIDE * SIDE + (z - along) % SIDE,
            (x - along) % SIDE * SIDE + (z - cross) % SIDE,
        )

    f0, f1, f2, f3 = [frames_at(d, ring) for d in range(SIDE)]
    bs, bw = band_start.reshape(-1), band_width

    pieces = pick(line[None], queries, key_rows, value_rows)
    pieces = [pieces[0]] + [line_shift(pieces[s], s) for s in range(1, SIDE)]

    other_weight = core_swap(out_weight)

    q, kv, k_last, v_last = stack(pieces)

    groups = [cross_shift(kv, s) for s in range(1, SIDE)]
    state = attend_line(f0, f0, bs, bw, q, kv, other_weight)

    here_and_across = frames_at(-ring, 0)
    *last_state, s_1, s_2, s_3 = attend_last_line(here_and_across, f0, bs, bw, queries, k_last, v_last, state[0])
    last = [cross_shift(sent, s) for s, sent in ((1, s_1), (2, s_2), (3, s_3))]

    state = attend_groups(f0, f1, bs, bw, q, groups[:1], state, False)
    o_main, token = attend_groups(f0, jnp.concatenate([f2, f3]), bs, bw, q, groups[1:], state, True)
    outs = [o_main[0]] + [line_shift(o_main[s], SIDE - s) for s in range(1, SIDE)]
    o_last = attend_bands(frame[None], jnp.concatenate([f1, f2, f3]), bs, bw, queries, last, last_state, token)
    outs.append(o_last[0])

    att = assemble(line[None], outs)
    att_other = core_swap(att)

    def share(ahead, *after):
        order = (y + jnp.array(ahead, jnp.int32)) % SIDE
        return project(order, core, att, att_other, out_weight, other_weight, *after)

    half = FT // 2
    two = share([2])
    from_down, from_up = y_shift(two[0, :half], 1), y_shift(two[0, half:], 3)
    near = share([1, 3], two)
    send_up, send_down = onward(near, from_down, from_up)
    own = share([0], near)
    return add(own[0], y_shift(send_up, 1), y_shift(send_down, 3))


def solution(mesh):
    return jax.shard_map(
        shards,
        mesh=mesh,
        in_specs=(
            P("frame", "head"),
            P("frame", "head"),
            P("frame", "head"),
            P("head", None),
            P(),
            P(),
        ),
        out_specs=P("frame", "head"),
        check_vma=False,
    )
```

```python
import functools

import jax
import jax.numpy as jnp
from jax import lax
from jax.experimental import pallas as pl
from jax.experimental.pallas import tpu as pltpu
from jax.sharding import PartitionSpec as P

HD = 128
BLOCK = 128
NB = 5
FT = 640
FRAMES = 16
SIDE = 4
ROWS = 128
LOG2_SCALE = 1.4426950408889634 / HD**0.5
NT = (((1,), (1,)), ((), ()))
NN = (((1,), (0,)), ((), ()))
BOTH = ("frame", "head")


def pairs(move):
    out = []
    for i in range(128):
        frame, head = divmod(i, 8)
        x, z, y, c = move(*divmod(frame, 4), *divmod(head, 2))
        out.append((i, (x % 4 * 4 + z % 4) * 8 + y % 4 * 2 + c))
    return out


def line_shift(v, s):
    return lax.ppermute(v, BOTH, pairs(lambda x, z, y, c: (x, z + s, y, c) if c == 0 else (x + s, z, y, c)))


def cross_shift(v, s):
    return lax.ppermute(v, BOTH, pairs(lambda x, z, y, c: (x + s, z, y, c) if c == 0 else (x, z + s, y, c)))


def y_shift(v, s):
    return lax.ppermute(v, BOTH, pairs(lambda x, z, y, c: (x, z, y + s, c)))


def core_swap(v):
    return lax.ppermute(v, BOTH, pairs(lambda x, z, y, c: (x, z, y, 1 - c)))


ANY = pl.BlockSpec(memory_space=pl.ANY)
VMEM = pl.BlockSpec(memory_space=pltpu.VMEM)
LIMIT = 20 << 20


def in_hbm(*arrays):
    return [pltpu.with_memory_space_constraint(v, pltpu.HBM) for v in arrays]


def pick_kernel(pos, q_any, k_any, v_any, *refs):
    outs, (q, k, v, sems) = refs[:SIDE], refs[SIDE:]
    rows = FT // 5
    copies = []
    for i in range(5):
        part = pl.ds(i * rows, rows)
        for j, (source, target) in enumerate(((q_any, q), (k_any, k), (v_any, v))):
            copies.append(pltpu.make_async_copy(source.at[part, :], target.at[part, :], sems.at[3 * i + j]))
    for copy in copies:
        copy.start()
    for i in range(5):
        for copy in copies[3 * i : 3 * i + 3]:
            copy.wait()
        part = slice(i * rows, (i + 1) * rows)
        for s, out in enumerate(outs):
            head = lax.rem(pos[0] + s, SIDE)
            columns = pl.ds(pl.multiple_of(head * HD, HD), HD)
            out[0, part, :] = q[part, columns]
            out[1, part, :] = k[part, columns]
            out[2, part, :] = v[part, columns]
            out[3, part, :] = k[part, 4 * HD :]
            out[4, part, :] = v[part, 4 * HD :]


def pick(pos, queries, keys, values):
    return pl.pallas_call(
        pick_kernel,
        in_specs=[pl.BlockSpec(memory_space=pltpu.SMEM)] + [ANY] * 3,
        out_specs=[VMEM] * SIDE,
        out_shape=[pltpu.VMEM((5, FT, HD), jnp.bfloat16)] * SIDE,
        scratch_shapes=[pltpu.VMEM((FT, 5 * HD), jnp.bfloat16)] * 3 + [pltpu.SemaphoreType.DMA((15,))],
        compiler_params=pltpu.CompilerParams(vmem_limit_bytes=LIMIT),
        name="pick",
    )(pos, *in_hbm(queries, keys, values))


def stack_kernel(parts, *refs):
    pieces, outs, sems = refs[:SIDE], refs[SIDE:-1], refs[-1]
    copies = []
    for out, rows in zip(outs, parts):
        for j, part in enumerate(rows):
            for s, piece in enumerate(pieces):
                copies.append(pltpu.make_async_copy(piece.at[part], out.at[j * SIDE + s], sems.at[len(copies)]))
    for copy in copies:
        copy.start()
    for copy in copies:
        copy.wait()


def stack(pieces, *parts):
    return pl.pallas_call(
        functools.partial(stack_kernel, parts),
        in_specs=[VMEM] * SIDE,
        out_specs=[ANY] * len(parts),
        out_shape=[pltpu.HBM((SIDE * len(rows), FT, HD), jnp.bfloat16) for rows in parts],
        scratch_shapes=[pltpu.SemaphoreType.DMA((SIDE * sum(map(len, parts)),))],
        compiler_params=pltpu.CompilerParams(vmem_limit_bytes=LIMIT),
        name="stack",
    )(*pieces)


def block_rows(n):
    return pl.ds(pl.multiple_of(n * BLOCK, BLOCK), BLOCK)


def place(n, keys, values, row, kc, vc, valid=None, stand_in=None):
    ones = lax.broadcasted_iota(jnp.int32, (BLOCK, HD), 1) == 0
    at = slice(n * BLOCK, (n + 1) * BLOCK)
    if valid is None:
        kc[at, :] = keys[block_rows(row), :]
        vc[at, 0:HD] = values[block_rows(row), :]
        vc[at, HD:] = ones.astype(jnp.bfloat16)
    else:
        kc[at, :] = keys[block_rows(jnp.where(valid, row, stand_in)), :]
        taken = values[block_rows(row), :]
        vc[at, 0:HD] = jnp.where(valid, taken, jnp.zeros_like(taken))
        vc[at, HD:] = jnp.where(ones & valid, 1.0, 0.0).astype(jnp.bfloat16)


def band_of(a, b, bs, bw):
    own = a == b
    first = jnp.where(own, 0, bs[a * FRAMES + b])
    second = jnp.where(first == NB - 1, 0, first + 1)
    return first, second, own | (bw[jnp.abs(a - b)] == 2)


def attend_to(q, kc, vc, state, emit):
    kk, vv = kc[...], vc[...]
    steps = FT // ROWS

    def score(r):
        return lax.dot_general(q[r * ROWS : (r + 1) * ROWS, :], kk, NT, preferred_element_type=jnp.float32)

    scores = score(0)
    for r in range(steps):
        later = score(r + 1) if r + 1 < steps else None
        rows = slice(r * ROWS, (r + 1) * ROWS)
        top = jnp.max(scores, axis=1, keepdims=True) * LOG2_SCALE
        if state:
            level = jnp.broadcast_to(state[1][0, r : r + 1, :], (ROWS, HD)).T[:, 0:1]
            top = jnp.maximum(top, level)
        probs = jnp.exp2(scores * LOG2_SCALE - top).astype(jnp.bfloat16)
        mixed = lax.dot_general(probs, vv, NN, preferred_element_type=jnp.float32)
        weighted, totals = mixed[:, 0:HD], mixed[:, HD : HD + 1]
        if state:
            share = jnp.exp2(level - top)
            weighted = weighted + state[0][0, rows, :].astype(jnp.float32) * share
            totals = totals + share
        emit(r, (weighted / totals).astype(jnp.bfloat16), top, totals)
        scores = later


def put_state(out, levels):
    def emit(r, result, top, totals):
        out[0, r * ROWS : (r + 1) * ROWS, :] = result
        level = top + jnp.log2(totals)
        levels[0, r : r + 1, :] = jnp.broadcast_to(level, (ROWS, HD)).T[0:1, :]

    return emit


def put_result(out):
    def emit(r, result, top, totals):
        out[0, r * ROWS : (r + 1) * ROWS, :] = result

    return emit


def line_kernel(qid, kid, bs, bw, q, kv, after, out, levels, kc, vc):
    del after
    i = pl.program_id(0)
    for s in range(SIDE):
        first, second, valid = band_of(qid[i], kid[s], bs, bw)
        place(2 * s, kv.at[s], kv.at[SIDE + s], first, kc, vc)
        place(2 * s + 1, kv.at[s], kv.at[SIDE + s], second, kc, vc, valid, first)
    for j in range(2, NB):
        place(2 * SIDE + j - 2, kv.at[i], kv.at[SIDE + i], j, kc, vc)
    attend_to(q.at[0], kc, vc, None, put_state(out, levels))


def last_line_kernel(qid, kid, bs, bw, q, keys, values, after, out, levels, s1, s2, s3, kc, vc):
    del after
    for s in range(SIDE):
        for i, sent in enumerate((s1, s2, s3)):
            first, second, unused = band_of(qid[i + 1], kid[s], bs, bw)
            for j, source in enumerate((keys, values)):
                sent[s, j, 0:BLOCK, :] = source[s, block_rows(first), :]
                sent[s, j, BLOCK:, :] = source[s, block_rows(second), :]
    for j in range(NB):
        place(j, keys.at[0], values.at[0], j, kc, vc)
    for s in range(1, SIDE):
        first, second, valid = band_of(qid[0], kid[s], bs, bw)
        n = NB + 2 * (s - 1)
        place(n, keys.at[s], values.at[s], first, kc, vc)
        place(n + 1, keys.at[s], values.at[s], second, kc, vc, valid, first)
    attend_to(q, kc, vc, None, put_state(out, levels))


ITEM = pl.BlockSpec((1, FT, HD), lambda i, *_: (i, 0, 0))
LEVEL = pl.BlockSpec((1, 8, HD), lambda i, *_: (i, 0, 0))


def cost(items, blocks):
    pairs_read = items * FT * blocks * BLOCK
    return pl.CostEstimate(flops=pairs_read * 4 * HD, bytes_accessed=8 << 20, transcendentals=pairs_read)


def packed(blocks):
    return [pltpu.VMEM((blocks * BLOCK, HD), jnp.bfloat16), pltpu.VMEM((blocks * BLOCK, 2 * HD), jnp.bfloat16)]


def state_shape(items):
    return [pltpu.HBM((items, FT, HD), jnp.bfloat16), pltpu.HBM((items, 8, HD), jnp.float32)]


def attend_line(qid, kid, bs, bw, q, kv, after):
    blocks = 2 * SIDE + NB - 2
    return pl.pallas_call(
        line_kernel,
        grid_spec=pltpu.PrefetchScalarGridSpec(
            num_scalar_prefetch=4,
            grid=(SIDE,),
            in_specs=[ITEM, pl.BlockSpec(kv.shape, lambda i, *_: (0, 0, 0)), ANY],
            out_specs=[ITEM, LEVEL],
            scratch_shapes=packed(blocks),
        ),
        out_shape=state_shape(SIDE),
        compiler_params=pltpu.CompilerParams(vmem_limit_bytes=LIMIT),
        cost_estimate=cost(SIDE, blocks),
        name="attend_line",
    )(qid, kid, bs, bw, *in_hbm(q, kv, after))


def attend_last_line(qid, kid, bs, bw, queries, keys, values, after):
    blocks = 2 * SIDE + NB - 2
    whole = pl.BlockSpec((SIDE, FT, HD), lambda i, *_: (0, 0, 0))
    sent = (SIDE, 2, 2 * BLOCK, HD)
    return pl.pallas_call(
        last_line_kernel,
        grid_spec=pltpu.PrefetchScalarGridSpec(
            num_scalar_prefetch=4,
            grid=(1,),
            in_specs=[pl.BlockSpec((FT, HD), lambda i, *_: (0, SIDE)), whole, whole, ANY],
            out_specs=[ITEM, LEVEL] + [pl.BlockSpec(sent, lambda i, *_: (0, 0, 0, 0))] * 3,
            scratch_shapes=packed(blocks),
        ),
        out_shape=state_shape(1) + [pltpu.HBM(sent, jnp.bfloat16)] * 3,
        compiler_params=pltpu.CompilerParams(vmem_limit_bytes=LIMIT),
        cost_estimate=cost(1, blocks),
        name="attend_last_line",
    )(qid, kid, bs, bw, *in_hbm(queries, keys, values, after))


def groups_kernel(count, finished, qid, kid, bs, bw, q, *refs):
    groups, (before, levels), results, (kc, vc) = refs[:count], refs[count : count + 2], refs[count + 2 : -2], refs[-2:]
    i = pl.program_id(0)
    for d, group in enumerate(groups):
        for s in range(SIDE):
            n = d * SIDE + s
            keys, values = group.at[s], group.at[SIDE + s]
            first, second, valid = band_of(qid[i], kid[n], bs, bw)
            place(2 * n, keys, values, first, kc, vc)
            place(2 * n + 1, keys, values, second, kc, vc, valid, first)
    if finished:
        out, token = results
        token[...] = jnp.zeros(token.shape, token.dtype)
        emit = put_result(out)
    else:
        emit = put_state(*results)
    attend_to(q.at[0], kc, vc, (before, levels), emit)


def attend_groups(qid, kid, bs, bw, q, groups, state, finished):
    blocks = 2 * SIDE * len(groups)
    if finished:
        out_specs = [ITEM, pl.BlockSpec((8, HD), lambda i, *_: (0, 0))]
        out_shape = [jax.ShapeDtypeStruct((SIDE, FT, HD), jnp.bfloat16), pltpu.HBM((8, HD), jnp.float32)]
    else:
        out_specs, out_shape = [ITEM, LEVEL], state_shape(SIDE)
    return pl.pallas_call(
        functools.partial(groups_kernel, len(groups), finished),
        grid_spec=pltpu.PrefetchScalarGridSpec(
            num_scalar_prefetch=4,
            grid=(SIDE,),
            in_specs=[ITEM] + [pl.BlockSpec(g.shape, lambda i, *_: (0, 0, 0)) for g in groups] + [ITEM, LEVEL],
            out_specs=out_specs,
            scratch_shapes=packed(blocks),
        ),
        out_shape=out_shape,
        compiler_params=pltpu.CompilerParams(vmem_limit_bytes=LIMIT),
        cost_estimate=cost(SIDE, blocks),
        name="attend_groups",
    )(qid, kid, bs, bw, *in_hbm(q), *groups, *in_hbm(*state))


def bands_attend_kernel(qid, kid, bs, bw, q, g1, g2, g3, before, levels, after, out, kc, vc):
    del after
    for d, group in enumerate((g1, g2, g3)):
        for s in range(SIDE):
            n = d * SIDE + s
            valid = band_of(qid[0], kid[n], bs, bw)[2]
            place(2 * n, group.at[s, 0], group.at[s, 1], 0, kc, vc)
            place(2 * n + 1, group.at[s, 0], group.at[s, 1], 1, kc, vc, valid, 0)
    attend_to(q, kc, vc, (before, levels), put_result(out))


def attend_bands(qid, kid, bs, bw, queries, groups, state, after):
    blocks = 2 * SIDE * len(groups)
    return pl.pallas_call(
        bands_attend_kernel,
        grid_spec=pltpu.PrefetchScalarGridSpec(
            num_scalar_prefetch=4,
            grid=(1,),
            in_specs=[pl.BlockSpec((FT, HD), lambda i, *_: (0, SIDE))]
            + [pl.BlockSpec(g.shape, lambda i, *_: (0, 0, 0, 0)) for g in groups]
            + [ITEM, LEVEL, ANY],
            out_specs=ITEM,
            scratch_shapes=packed(blocks),
        ),
        out_shape=jax.ShapeDtypeStruct((1, FT, HD), jnp.bfloat16),
        compiler_params=pltpu.CompilerParams(vmem_limit_bytes=LIMIT),
        cost_estimate=cost(1, blocks),
        name="attend_bands",
    )(qid, kid, bs, bw, *in_hbm(queries), *groups, *in_hbm(*state, after))


def assemble_kernel(pos, o0, o1, o2, o3, o4, att):
    for s, o in enumerate((o0, o1, o2, o3)):
        head = lax.rem(pos[0] + s, SIDE)
        att[:, pl.ds(pl.multiple_of(head * HD, HD), HD)] = o[...]
    att[:, SIDE * HD :] = o4[...]


def assemble(pos, outs):
    return pl.pallas_call(
        assemble_kernel,
        in_specs=[pl.BlockSpec(memory_space=pltpu.SMEM)] + [VMEM] * 5,
        out_specs=VMEM,
        out_shape=jax.ShapeDtypeStruct((FT, 5 * HD), jnp.bfloat16),
        compiler_params=pltpu.CompilerParams(vmem_limit_bytes=LIMIT),
        name="assemble",
    )(pos, *outs)


def project_kernel(order, blocks, att, att_other, w_mine, w_other, *refs):
    del order, blocks
    out, step = refs[-1], FT // 2
    for r in range(0, FT, step):
        rows = slice(r, r + step)
        total = jnp.dot(att[rows, :], w_mine[...], preferred_element_type=jnp.float32)
        total = total + jnp.dot(att_other[rows, :], w_other[...], preferred_element_type=jnp.float32)
        out[pl.program_id(0), rows, :] = total.astype(jnp.bfloat16)


def project(order, core, att, att_other, weight, other_weight, *after):
    count, width = order.shape[0], weight.shape[1] // 8
    return pl.pallas_call(
        project_kernel,
        grid_spec=pltpu.PrefetchScalarGridSpec(
            num_scalar_prefetch=2,
            grid=(count,),
            in_specs=[
                VMEM,
                VMEM,
                pl.BlockSpec((5 * HD, width), lambda i, order, blocks: (0, blocks[i])),
                pl.BlockSpec((5 * HD, width), lambda i, order, blocks: (0, blocks[i])),
            ]
            + [ANY] * len(after),
            out_specs=VMEM,
        ),
        out_shape=jax.ShapeDtypeStruct((count, FT, width), jnp.bfloat16),
        compiler_params=pltpu.CompilerParams(vmem_limit_bytes=LIMIT),
        name="project",
    )(order, 2 * order + core, att, att_other, *in_hbm(weight, other_weight), *after)


def first_share_kernel(blocks, att, weight, other, base, later):
    del blocks
    base[...] = jnp.dot(att[...], weight[...], preferred_element_type=jnp.float32)
    later[...] = other[...]


def first_share(blocks, att, weight, other_weight):
    width = weight.shape[1] // 8
    block = pl.BlockSpec((5 * HD, width), lambda i, blocks: (0, blocks[0]))
    return pl.pallas_call(
        first_share_kernel,
        grid_spec=pltpu.PrefetchScalarGridSpec(
            num_scalar_prefetch=1, grid=(1,), in_specs=[VMEM, block, block], out_specs=[VMEM] * 2
        ),
        out_shape=[pltpu.VMEM((FT, width), jnp.float32), pltpu.VMEM((5 * HD, width), jnp.bfloat16)],
        compiler_params=pltpu.CompilerParams(vmem_limit_bytes=LIMIT),
        name="first_share",
    )(blocks, att, *in_hbm(weight, other_weight))


def second_share_kernel(att_other, base, weight, out):
    total = base[...] + jnp.dot(att_other[...], weight[...], preferred_element_type=jnp.float32)
    out[...] = total.astype(jnp.bfloat16)


def second_share(att_other, base, weight):
    return pl.pallas_call(
        second_share_kernel,
        in_specs=[VMEM] * 3,
        out_specs=VMEM,
        out_shape=pltpu.VMEM(base.shape, jnp.bfloat16),
        compiler_params=pltpu.CompilerParams(vmem_limit_bytes=LIMIT),
        name="second_share",
    )(att_other, base, weight)


def add(*terms):
    total = terms[0].astype(jnp.float32)
    for t in terms[1:]:
        total = total + t.astype(jnp.float32)
    return total.astype(jnp.bfloat16)


def onward_kernel(near, from_down, from_up, send_up, send_down):
    half = FT // 2
    wide = lambda v: v.astype(jnp.float32)
    send_up[0:half, :] = (wide(near[0, 0:half, :]) + wide(from_down[...])).astype(jnp.bfloat16)
    send_up[half:, :] = near[0, half:, :]
    send_down[0:half, :] = near[1, 0:half, :]
    send_down[half:, :] = (wide(near[1, half:, :]) + wide(from_up[...])).astype(jnp.bfloat16)


def onward(near, from_down, from_up):
    return pl.pallas_call(
        onward_kernel,
        in_specs=[VMEM] * 3,
        out_specs=[VMEM] * 2,
        out_shape=[jax.ShapeDtypeStruct(near.shape[1:], jnp.bfloat16)] * 2,
        compiler_params=pltpu.CompilerParams(vmem_limit_bytes=LIMIT),
        name="onward",
    )(near, from_down, from_up)


def shards(queries, key_rows, value_rows, out_weight, band_start, band_width):
    frame, head = lax.axis_index("frame"), lax.axis_index("head")
    x, z = frame // SIDE, frame % SIDE
    y, core = head // 2, head % 2
    line = jnp.where(core == 0, z, x)
    ring = jnp.arange(SIDE, dtype=jnp.int32)

    def frames_at(cross, along):
        return jnp.where(
            core == 0,
            (x - cross) % SIDE * SIDE + (z - along) % SIDE,
            (x - along) % SIDE * SIDE + (z - cross) % SIDE,
        )

    f0, f1, f2, f3 = [frames_at(d, ring) for d in range(SIDE)]
    bs, bw = band_start.reshape(-1), band_width

    pieces = pick(line[None], queries, key_rows, value_rows)
    one, three = line_shift(pieces[1], 1), line_shift(pieces[3], 3)
    pieces = [pieces[0], one, line_shift(pieces[2], 2), three]

    other_weight = core_swap(out_weight)

    (kv,) = stack(pieces, (1, 2))
    q, k_last, v_last = stack(pieces, (0,), (3,), (4,))

    groups = [cross_shift(kv, s) for s in range(1, SIDE)]
    state = attend_line(f0, f0, bs, bw, q, kv, other_weight)

    here_and_across = frames_at(-ring, 0)
    *last_state, s_1, s_2, s_3 = attend_last_line(here_and_across, f0, bs, bw, queries, k_last, v_last, state[0])
    last = [cross_shift(sent, s) for s, sent in ((1, s_1), (2, s_2), (3, s_3))]

    state = attend_groups(f0, f1, bs, bw, q, groups[:1], state, False)
    o_main, token = attend_groups(f0, jnp.concatenate([f2, f3]), bs, bw, q, groups[1:], state, True)
    outs = [o_main[0]] + [line_shift(o_main[s], SIDE - s) for s in range(1, SIDE)]
    o_last = attend_bands(frame[None], jnp.concatenate([f1, f2, f3]), bs, bw, queries, last, last_state, token)
    outs.append(o_last[0])

    att = assemble(line[None], outs)
    att_other = core_swap(att)

    def share(ahead, *after):
        order = (y + jnp.array(ahead, jnp.int32)) % SIDE
        return project(order, core, att, att_other, out_weight, other_weight, *after)

    half = FT // 2
    far = (y[None] + 2) % SIDE * 2 + core
    two = second_share(att_other, *first_share(far, att, out_weight, other_weight))
    from_down, from_up = y_shift(two[:half], 1), y_shift(two[half:], 3)
    near = share([1, 3], two)
    send_up, send_down = onward(near, from_down, from_up)
    own = share([0], near)
    return add(own[0], y_shift(send_up, 1), y_shift(send_down, 3))


def solution(mesh):
    return jax.shard_map(
        shards,
        mesh=mesh,
        in_specs=(
            P("frame", "head"),
            P("frame", "head"),
            P("frame", "head"),
            P("head", None),
            P(),
            P(),
        ),
        out_specs=P("frame", "head"),
        check_vma=False,
    )
```

```python
import functools

import jax
import jax.numpy as jnp
from jax import lax
from jax.experimental import pallas as pl
from jax.experimental.pallas import tpu as pltpu
from jax.sharding import PartitionSpec as P

HD = 128
BLOCK = 128
NB = 5
FT = 640
FRAMES = 16
SIDE = 4
ROWS = 128
LOG2_SCALE = 1.4426950408889634 / HD**0.5
NT = (((1,), (1,)), ((), ()))
NN = (((1,), (0,)), ((), ()))
BOTH = ("frame", "head")


def pairs(move):
    out = []
    for i in range(128):
        frame, head = divmod(i, 8)
        x, z, y, c = move(*divmod(frame, 4), *divmod(head, 2))
        out.append((i, (x % 4 * 4 + z % 4) * 8 + y % 4 * 2 + c))
    return out


def line_shift(v, s):
    return lax.ppermute(v, BOTH, pairs(lambda x, z, y, c: (x, z + s, y, c) if c == 0 else (x + s, z, y, c)))


def cross_shift(v, s):
    return lax.ppermute(v, BOTH, pairs(lambda x, z, y, c: (x + s, z, y, c) if c == 0 else (x, z + s, y, c)))


def y_shift(v, s):
    return lax.ppermute(v, BOTH, pairs(lambda x, z, y, c: (x, z, y + s, c)))


def core_swap(v):
    return lax.ppermute(v, BOTH, pairs(lambda x, z, y, c: (x, z, y, 1 - c)))


ANY = pl.BlockSpec(memory_space=pl.ANY)
VMEM = pl.BlockSpec(memory_space=pltpu.VMEM)
LIMIT = 20 << 20


def in_hbm(*arrays):
    return [pltpu.with_memory_space_constraint(v, pltpu.HBM) for v in arrays]


def pick_kernel(pos, q_any, k_any, v_any, *refs):
    outs, (q, k, v, sems) = refs[:SIDE], refs[SIDE:]
    rows = FT // 5
    copies = []
    for i in range(5):
        part = pl.ds(i * rows, rows)
        for j, (source, target) in enumerate(((q_any, q), (k_any, k), (v_any, v))):
            copies.append(pltpu.make_async_copy(source.at[part, :], target.at[part, :], sems.at[3 * i + j]))
    for copy in copies:
        copy.start()
    for i in range(5):
        for copy in copies[3 * i : 3 * i + 3]:
            copy.wait()
        part = slice(i * rows, (i + 1) * rows)
        for s, out in enumerate(outs):
            head = lax.rem(pos[0] + s, SIDE)
            columns = pl.ds(pl.multiple_of(head * HD, HD), HD)
            out[0, part, :] = q[part, columns]
            out[1, part, :] = k[part, columns]
            out[2, part, :] = v[part, columns]
            out[3, part, :] = k[part, 4 * HD :]
            out[4, part, :] = v[part, 4 * HD :]


def pick(pos, queries, keys, values):
    return pl.pallas_call(
        pick_kernel,
        in_specs=[pl.BlockSpec(memory_space=pltpu.SMEM)] + [ANY] * 3,
        out_specs=[VMEM] * SIDE,
        out_shape=[pltpu.VMEM((5, FT, HD), jnp.bfloat16)] * SIDE,
        scratch_shapes=[pltpu.VMEM((FT, 5 * HD), jnp.bfloat16)] * 3 + [pltpu.SemaphoreType.DMA((15,))],
        compiler_params=pltpu.CompilerParams(vmem_limit_bytes=LIMIT),
        name="pick",
    )(pos, *in_hbm(queries, keys, values))


def stack_kernel(parts, *refs):
    pieces, outs, sems = refs[:SIDE], refs[SIDE:-1], refs[-1]
    copies = []
    for out, rows in zip(outs, parts):
        for j, part in enumerate(rows):
            for s, piece in enumerate(pieces):
                copies.append(pltpu.make_async_copy(piece.at[part], out.at[j * SIDE + s], sems.at[len(copies)]))
    for copy in copies:
        copy.start()
    for copy in copies:
        copy.wait()


def stack(pieces, *parts):
    return pl.pallas_call(
        functools.partial(stack_kernel, parts),
        in_specs=[VMEM] * SIDE,
        out_specs=[ANY] * len(parts),
        out_shape=[pltpu.HBM((SIDE * len(rows), FT, HD), jnp.bfloat16) for rows in parts],
        scratch_shapes=[pltpu.SemaphoreType.DMA((SIDE * sum(map(len, parts)),))],
        compiler_params=pltpu.CompilerParams(vmem_limit_bytes=LIMIT),
        name="stack",
    )(*pieces)


def block_rows(n):
    return pl.ds(pl.multiple_of(n * BLOCK, BLOCK), BLOCK)


def place(n, keys, values, row, kc, vc, valid=None, stand_in=None):
    ones = lax.broadcasted_iota(jnp.int32, (BLOCK, HD), 1) == 0
    at = slice(n * BLOCK, (n + 1) * BLOCK)
    if valid is None:
        kc[at, :] = keys[block_rows(row), :]
        vc[at, 0:HD] = values[block_rows(row), :]
        vc[at, HD:] = ones.astype(jnp.bfloat16)
    else:
        kc[at, :] = keys[block_rows(jnp.where(valid, row, stand_in)), :]
        taken = values[block_rows(row), :]
        vc[at, 0:HD] = jnp.where(valid, taken, jnp.zeros_like(taken))
        vc[at, HD:] = jnp.where(ones & valid, 1.0, 0.0).astype(jnp.bfloat16)


def band_of(a, b, bs, bw):
    own = a == b
    first = jnp.where(own, 0, bs[a * FRAMES + b])
    second = jnp.where(first == NB - 1, 0, first + 1)
    return first, second, own | (bw[jnp.abs(a - b)] == 2)


def attend_to(q, kc, vc, state, emit):
    kk, vv = kc[...], vc[...]
    steps = FT // ROWS

    def score(r):
        return lax.dot_general(q[r * ROWS : (r + 1) * ROWS, :], kk, NT, preferred_element_type=jnp.float32)

    scores = score(0)
    for r in range(steps):
        later = score(r + 1) if r + 1 < steps else None
        rows = slice(r * ROWS, (r + 1) * ROWS)
        top = jnp.max(scores, axis=1, keepdims=True) * LOG2_SCALE
        if state:
            level = state[1][0, rows, 0:1]
            top = jnp.maximum(top, level)
        probs = jnp.exp2(scores * LOG2_SCALE - top).astype(jnp.bfloat16)
        mixed = lax.dot_general(probs, vv, NN, preferred_element_type=jnp.float32)
        weighted, totals = mixed[:, 0:HD], mixed[:, HD : HD + 1]
        if state:
            share = jnp.exp2(level - top)
            weighted = weighted + state[0][0, rows, :].astype(jnp.float32) * share
            totals = totals + share
        emit(r, (weighted / totals).astype(jnp.bfloat16), top, totals)
        scores = later


def put_state(out, levels):
    def emit(r, result, top, totals):
        rows = slice(r * ROWS, (r + 1) * ROWS)
        out[0, rows, :] = result
        levels[0, rows, :] = jnp.broadcast_to(top + jnp.log2(totals), (ROWS, HD))

    return emit


def put_result(out):
    def emit(r, result, top, totals):
        out[0, r * ROWS : (r + 1) * ROWS, :] = result

    return emit


def line_kernel(qid, kid, bs, bw, q, kv, after, out, levels, kc, vc):
    del after
    i = pl.program_id(0)
    for s in range(SIDE):
        first, second, valid = band_of(qid[i], kid[s], bs, bw)
        place(2 * s, kv.at[s], kv.at[SIDE + s], first, kc, vc)
        place(2 * s + 1, kv.at[s], kv.at[SIDE + s], second, kc, vc, valid, first)
    for j in range(2, NB):
        place(2 * SIDE + j - 2, kv.at[i], kv.at[SIDE + i], j, kc, vc)
    attend_to(q.at[0], kc, vc, None, put_state(out, levels))


def last_line_kernel(qid, kid, bs, bw, q, keys, values, after, out, levels, s1, s2, s3, kc, vc):
    del after
    for s in range(SIDE):
        for i, sent in enumerate((s1, s2, s3)):
            first, second, unused = band_of(qid[i + 1], kid[s], bs, bw)
            for j, source in enumerate((keys, values)):
                sent[s, j, 0:BLOCK, :] = source[s, block_rows(first), :]
                sent[s, j, BLOCK:, :] = source[s, block_rows(second), :]
    for j in range(NB):
        place(j, keys.at[0], values.at[0], j, kc, vc)
    for s in range(1, SIDE):
        first, second, valid = band_of(qid[0], kid[s], bs, bw)
        n = NB + 2 * (s - 1)
        place(n, keys.at[s], values.at[s], first, kc, vc)
        place(n + 1, keys.at[s], values.at[s], second, kc, vc, valid, first)
    attend_to(q, kc, vc, None, put_state(out, levels))


ITEM = pl.BlockSpec((1, FT, HD), lambda i, *_: (i, 0, 0))


def cost(items, blocks):
    pairs_read = items * FT * blocks * BLOCK
    return pl.CostEstimate(flops=pairs_read * 4 * HD, bytes_accessed=8 << 20, transcendentals=pairs_read)


def packed(blocks):
    return [pltpu.VMEM((blocks * BLOCK, HD), jnp.bfloat16), pltpu.VMEM((blocks * BLOCK, 2 * HD), jnp.bfloat16)]


def state_shape(items):
    return [pltpu.HBM((items, FT, HD), jnp.bfloat16), pltpu.HBM((items, FT, HD), jnp.float32)]


def attend_line(qid, kid, bs, bw, q, kv, after):
    blocks = 2 * SIDE + NB - 2
    return pl.pallas_call(
        line_kernel,
        grid_spec=pltpu.PrefetchScalarGridSpec(
            num_scalar_prefetch=4,
            grid=(SIDE,),
            in_specs=[ITEM, pl.BlockSpec(kv.shape, lambda i, *_: (0, 0, 0)), ANY],
            out_specs=[ITEM, ITEM],
            scratch_shapes=packed(blocks),
        ),
        out_shape=state_shape(SIDE),
        compiler_params=pltpu.CompilerParams(vmem_limit_bytes=LIMIT),
        cost_estimate=cost(SIDE, blocks),
        name="attend_line",
    )(qid, kid, bs, bw, *in_hbm(q, kv, after))


def attend_last_line(qid, kid, bs, bw, queries, keys, values, after):
    blocks = 2 * SIDE + NB - 2
    whole = pl.BlockSpec((SIDE, FT, HD), lambda i, *_: (0, 0, 0))
    sent = (SIDE, 2, 2 * BLOCK, HD)
    return pl.pallas_call(
        last_line_kernel,
        grid_spec=pltpu.PrefetchScalarGridSpec(
            num_scalar_prefetch=4,
            grid=(1,),
            in_specs=[pl.BlockSpec((FT, HD), lambda i, *_: (0, SIDE)), whole, whole, ANY],
            out_specs=[ITEM, ITEM] + [pl.BlockSpec(sent, lambda i, *_: (0, 0, 0, 0))] * 3,
            scratch_shapes=packed(blocks),
        ),
        out_shape=state_shape(1) + [pltpu.HBM(sent, jnp.bfloat16)] * 3,
        compiler_params=pltpu.CompilerParams(vmem_limit_bytes=LIMIT),
        cost_estimate=cost(1, blocks),
        name="attend_last_line",
    )(qid, kid, bs, bw, *in_hbm(queries, keys, values, after))


def groups_kernel(count, finished, qid, kid, bs, bw, q, *refs):
    groups, (before, levels), results, (kc, vc) = refs[:count], refs[count : count + 2], refs[count + 2 : -2], refs[-2:]
    i = pl.program_id(0)
    for d, group in enumerate(groups):
        for s in range(SIDE):
            n = d * SIDE + s
            keys, values = group.at[s], group.at[SIDE + s]
            first, second, valid = band_of(qid[i], kid[n], bs, bw)
            place(2 * n, keys, values, first, kc, vc)
            place(2 * n + 1, keys, values, second, kc, vc, valid, first)
    if finished:
        out, token = results
        token[...] = jnp.zeros(token.shape, token.dtype)
        emit = put_result(out)
    else:
        emit = put_state(*results)
    attend_to(q.at[0], kc, vc, (before, levels), emit)


def attend_groups(qid, kid, bs, bw, q, groups, state, finished):
    blocks = 2 * SIDE * len(groups)
    if finished:
        out_specs = [ITEM, pl.BlockSpec((8, HD), lambda i, *_: (0, 0))]
        out_shape = [jax.ShapeDtypeStruct((SIDE, FT, HD), jnp.bfloat16), pltpu.HBM((8, HD), jnp.float32)]
    else:
        out_specs, out_shape = [ITEM, ITEM], state_shape(SIDE)
    return pl.pallas_call(
        functools.partial(groups_kernel, len(groups), finished),
        grid_spec=pltpu.PrefetchScalarGridSpec(
            num_scalar_prefetch=4,
            grid=(SIDE,),
            in_specs=[ITEM] + [pl.BlockSpec(g.shape, lambda i, *_: (0, 0, 0)) for g in groups] + [ITEM, ITEM],
            out_specs=out_specs,
            scratch_shapes=packed(blocks),
        ),
        out_shape=out_shape,
        compiler_params=pltpu.CompilerParams(vmem_limit_bytes=LIMIT),
        cost_estimate=cost(SIDE, blocks),
        name="attend_groups",
    )(qid, kid, bs, bw, *in_hbm(q), *groups, *in_hbm(*state))


def bands_attend_kernel(qid, kid, bs, bw, q, g1, g2, g3, before, levels, after, out, kc, vc):
    del after
    for d, group in enumerate((g1, g2, g3)):
        for s in range(SIDE):
            n = d * SIDE + s
            valid = band_of(qid[0], kid[n], bs, bw)[2]
            place(2 * n, group.at[s, 0], group.at[s, 1], 0, kc, vc)
            place(2 * n + 1, group.at[s, 0], group.at[s, 1], 1, kc, vc, valid, 0)
    attend_to(q, kc, vc, (before, levels), put_result(out))


def attend_bands(qid, kid, bs, bw, queries, groups, state, after):
    blocks = 2 * SIDE * len(groups)
    return pl.pallas_call(
        bands_attend_kernel,
        grid_spec=pltpu.PrefetchScalarGridSpec(
            num_scalar_prefetch=4,
            grid=(1,),
            in_specs=[pl.BlockSpec((FT, HD), lambda i, *_: (0, SIDE))]
            + [pl.BlockSpec(g.shape, lambda i, *_: (0, 0, 0, 0)) for g in groups]
            + [ITEM, ITEM, ANY],
            out_specs=ITEM,
            scratch_shapes=packed(blocks),
        ),
        out_shape=jax.ShapeDtypeStruct((1, FT, HD), jnp.bfloat16),
        compiler_params=pltpu.CompilerParams(vmem_limit_bytes=LIMIT),
        cost_estimate=cost(1, blocks),
        name="attend_bands",
    )(qid, kid, bs, bw, *in_hbm(queries), *groups, *in_hbm(*state, after))


def assemble_kernel(pos, o0, o1, o2, o3, o4, att):
    for s, o in enumerate((o0, o1, o2, o3)):
        head = lax.rem(pos[0] + s, SIDE)
        att[:, pl.ds(pl.multiple_of(head * HD, HD), HD)] = o[...]
    att[:, SIDE * HD :] = o4[...]


def assemble(pos, outs):
    return pl.pallas_call(
        assemble_kernel,
        in_specs=[pl.BlockSpec(memory_space=pltpu.SMEM)] + [VMEM] * 5,
        out_specs=VMEM,
        out_shape=jax.ShapeDtypeStruct((FT, 5 * HD), jnp.bfloat16),
        compiler_params=pltpu.CompilerParams(vmem_limit_bytes=LIMIT),
        name="assemble",
    )(pos, *outs)


def project_kernel(order, blocks, att, att_other, w_mine, w_other, *refs):
    del order, blocks
    out, step = refs[-1], FT // 2
    for r in range(0, FT, step):
        rows = slice(r, r + step)
        total = jnp.dot(att[rows, :], w_mine[...], preferred_element_type=jnp.float32)
        total = total + jnp.dot(att_other[rows, :], w_other[...], preferred_element_type=jnp.float32)
        out[pl.program_id(0), rows, :] = total.astype(jnp.bfloat16)


def project(order, core, att, att_other, weight, other_weight, *after):
    count, width = order.shape[0], weight.shape[1] // 8
    return pl.pallas_call(
        project_kernel,
        grid_spec=pltpu.PrefetchScalarGridSpec(
            num_scalar_prefetch=2,
            grid=(count,),
            in_specs=[
                VMEM,
                VMEM,
                pl.BlockSpec((5 * HD, width), lambda i, order, blocks: (0, blocks[i])),
                pl.BlockSpec((5 * HD, width), lambda i, order, blocks: (0, blocks[i])),
            ]
            + [ANY] * len(after),
            out_specs=VMEM,
        ),
        out_shape=jax.ShapeDtypeStruct((count, FT, width), jnp.bfloat16),
        compiler_params=pltpu.CompilerParams(vmem_limit_bytes=LIMIT),
        name="project",
    )(order, 2 * order + core, att, att_other, *in_hbm(weight, other_weight), *after)


def first_share_kernel(blocks, att, weight, other, base, later):
    del blocks
    base[...] = jnp.dot(att[...], weight[...], preferred_element_type=jnp.float32)
    later[...] = other[...]


def first_share(blocks, att, weight, other_weight):
    width = weight.shape[1] // 8
    block = pl.BlockSpec((5 * HD, width), lambda i, blocks: (0, blocks[0]))
    return pl.pallas_call(
        first_share_kernel,
        grid_spec=pltpu.PrefetchScalarGridSpec(
            num_scalar_prefetch=1, grid=(1,), in_specs=[VMEM, block, block], out_specs=[VMEM] * 2
        ),
        out_shape=[pltpu.VMEM((FT, width), jnp.float32), pltpu.VMEM((5 * HD, width), jnp.bfloat16)],
        compiler_params=pltpu.CompilerParams(vmem_limit_bytes=LIMIT),
        name="first_share",
    )(blocks, att, *in_hbm(weight, other_weight))


def second_share_kernel(att_other, base, weight, out):
    total = base[...] + jnp.dot(att_other[...], weight[...], preferred_element_type=jnp.float32)
    out[...] = total.astype(jnp.bfloat16)


def second_share(att_other, base, weight):
    return pl.pallas_call(
        second_share_kernel,
        in_specs=[VMEM] * 3,
        out_specs=VMEM,
        out_shape=pltpu.VMEM(base.shape, jnp.bfloat16),
        compiler_params=pltpu.CompilerParams(vmem_limit_bytes=LIMIT),
        name="second_share",
    )(att_other, base, weight)


def add(*terms):
    total = terms[0].astype(jnp.float32)
    for t in terms[1:]:
        total = total + t.astype(jnp.float32)
    return total.astype(jnp.bfloat16)


def onward_kernel(near, from_down, from_up, send_up, send_down):
    half = FT // 2
    wide = lambda v: v.astype(jnp.float32)
    send_up[...] = (wide(near[0, 0:half, :]) + wide(from_down[...])).astype(jnp.bfloat16)
    send_down[...] = (wide(near[1, half:, :]) + wide(from_up[...])).astype(jnp.bfloat16)


def onward(near, from_down, from_up):
    return pl.pallas_call(
        onward_kernel,
        in_specs=[VMEM] * 3,
        out_specs=[VMEM] * 2,
        out_shape=[jax.ShapeDtypeStruct(from_up.shape, jnp.bfloat16)] * 2,
        compiler_params=pltpu.CompilerParams(vmem_limit_bytes=LIMIT),
        name="onward",
    )(near, from_down, from_up)


def finish_kernel(own, more_up, plain_up, more_down, plain_down, out):
    half = FT // 2
    wide = lambda v: v.astype(jnp.float32)
    out[0:half, :] = (wide(own[0:half, :]) + wide(more_up[...]) + wide(plain_down[...])).astype(jnp.bfloat16)
    out[half:, :] = (wide(own[half:, :]) + wide(more_down[...]) + wide(plain_up[...])).astype(jnp.bfloat16)


def finish(*args):
    return pl.pallas_call(
        finish_kernel,
        in_specs=[VMEM] * 5,
        out_specs=pl.BlockSpec(args[0].shape, lambda: (0, 0)),
        out_shape=jax.ShapeDtypeStruct(args[0].shape, jnp.bfloat16),
        compiler_params=pltpu.CompilerParams(vmem_limit_bytes=LIMIT),
        name="finish",
    )(*args)


def shards(queries, key_rows, value_rows, out_weight, band_start, band_width):
    frame, head = lax.axis_index("frame"), lax.axis_index("head")
    x, z = frame // SIDE, frame % SIDE
    y, core = head // 2, head % 2
    line = jnp.where(core == 0, z, x)
    ring = jnp.arange(SIDE, dtype=jnp.int32)

    def frames_at(cross, along):
        return jnp.where(
            core == 0,
            (x - cross) % SIDE * SIDE + (z - along) % SIDE,
            (x - along) % SIDE * SIDE + (z - cross) % SIDE,
        )

    f0, f1, f2, f3 = [frames_at(d, ring) for d in range(SIDE)]
    bs, bw = band_start.reshape(-1), band_width

    pieces = pick(line[None], queries, key_rows, value_rows)
    one, three = line_shift(pieces[1], 1), line_shift(pieces[3], 3)
    pieces = [pieces[0], one, line_shift(pieces[2], 2), three]

    other_weight = core_swap(out_weight)

    (kv,) = stack(pieces, (1, 2))
    q, k_last, v_last = stack(pieces, (0,), (3,), (4,))

    groups = [cross_shift(kv, s) for s in range(1, SIDE)]
    state = attend_line(f0, f0, bs, bw, q, kv, other_weight)

    here_and_across = frames_at(-ring, 0)
    *last_state, s_1, s_2, s_3 = attend_last_line(here_and_across, f0, bs, bw, queries, k_last, v_last, state[0])
    last = [cross_shift(sent, s) for s, sent in ((1, s_1), (2, s_2), (3, s_3))]

    state = attend_groups(f0, f1, bs, bw, q, groups[:1], state, False)
    o_main, token = attend_groups(f0, jnp.concatenate([f2, f3]), bs, bw, q, groups[1:], state, True)
    outs = [o_main[0]] + [line_shift(o_main[s], SIDE - s) for s in range(1, SIDE)]
    o_last = attend_bands(frame[None], jnp.concatenate([f1, f2, f3]), bs, bw, queries, last, last_state, token)
    outs.append(o_last[0])

    att = assemble(line[None], outs)
    att_other = core_swap(att)

    def share(ahead, *after):
        order = (y + jnp.array(ahead, jnp.int32)) % SIDE
        return project(order, core, att, att_other, out_weight, other_weight, *after)

    half = FT // 2
    far = (y[None] + 2) % SIDE * 2 + core
    two = second_share(att_other, *first_share(far, att, out_weight, other_weight))
    from_down, from_up = y_shift(two[:half], 1), y_shift(two[half:], 3)
    near = share([1, 3], two)
    plain_up, plain_down = y_shift(near[0, half:], 1), y_shift(near[1, :half], 3)
    send_up, send_down = onward(near, from_down, from_up)
    own = share([0], near)
    return finish(own[0], y_shift(send_up, 1), plain_up, y_shift(send_down, 3), plain_down)


def solution(mesh):
    return jax.shard_map(
        shards,
        mesh=mesh,
        in_specs=(
            P("frame", "head"),
            P("frame", "head"),
            P("frame", "head"),
            P("head", None),
            P(),
            P(),
        ),
        out_specs=P("frame", "head"),
        check_vma=False,
    )
```

```python
import functools

import jax
import jax.numpy as jnp
from jax import lax
from jax.experimental import pallas as pl
from jax.experimental.pallas import tpu as pltpu
from jax.sharding import PartitionSpec as P

HD = 128
BLOCK = 128
NB = 5
FT = 640
FRAMES = 16
SIDE = 4
ROWS = 320
LOG2_SCALE = 1.4426950408889634 / HD**0.5
NT = (((1,), (1,)), ((), ()))
NN = (((1,), (0,)), ((), ()))
BOTH = ("frame", "head")


def pairs(move):
    out = []
    for i in range(128):
        frame, head = divmod(i, 8)
        x, z, y, c = move(*divmod(frame, 4), *divmod(head, 2))
        out.append((i, (x % 4 * 4 + z % 4) * 8 + y % 4 * 2 + c))
    return out


def line_shift(v, s):
    return lax.ppermute(v, BOTH, pairs(lambda x, z, y, c: (x, z + s, y, c) if c == 0 else (x + s, z, y, c)))


def cross_shift(v, s):
    return lax.ppermute(v, BOTH, pairs(lambda x, z, y, c: (x + s, z, y, c) if c == 0 else (x, z + s, y, c)))


def y_shift(v, s):
    return lax.ppermute(v, BOTH, pairs(lambda x, z, y, c: (x, z, y + s, c)))


def core_swap(v):
    return lax.ppermute(v, BOTH, pairs(lambda x, z, y, c: (x, z, y, 1 - c)))


ANY = pl.BlockSpec(memory_space=pl.ANY)
VMEM = pl.BlockSpec(memory_space=pltpu.VMEM)
LIMIT = 20 << 20


def in_hbm(*arrays):
    return [pltpu.with_memory_space_constraint(v, pltpu.HBM) for v in arrays]


def pick_kernel(pos, q_any, k_any, v_any, *refs):
    outs, (q, k, v, sems) = refs[:SIDE], refs[SIDE:]
    rows = FT // 5
    copies = []
    for i in range(5):
        part = pl.ds(i * rows, rows)
        for j, (source, target) in enumerate(((q_any, q), (k_any, k), (v_any, v))):
            copies.append(pltpu.make_async_copy(source.at[part, :], target.at[part, :], sems.at[3 * i + j]))
    for copy in copies:
        copy.start()
    for i in range(5):
        for copy in copies[3 * i : 3 * i + 3]:
            copy.wait()
        part = slice(i * rows, (i + 1) * rows)
        for s, out in enumerate(outs):
            head = lax.rem(pos[0] + s, SIDE)
            columns = pl.ds(pl.multiple_of(head * HD, HD), HD)
            out[0, part, :] = q[part, columns]
            out[1, part, :] = k[part, columns]
            out[2, part, :] = v[part, columns]
            out[3, part, :] = k[part, 4 * HD :]
            out[4, part, :] = v[part, 4 * HD :]


def pick(pos, queries, keys, values):
    return pl.pallas_call(
        pick_kernel,
        in_specs=[pl.BlockSpec(memory_space=pltpu.SMEM)] + [ANY] * 3,
        out_specs=[VMEM] * SIDE,
        out_shape=[pltpu.VMEM((5, FT, HD), jnp.bfloat16)] * SIDE,
        scratch_shapes=[pltpu.VMEM((FT, 5 * HD), jnp.bfloat16)] * 3 + [pltpu.SemaphoreType.DMA((15,))],
        compiler_params=pltpu.CompilerParams(vmem_limit_bytes=LIMIT),
        name="pick",
    )(pos, *in_hbm(queries, keys, values))


def stack_kernel(parts, *refs):
    pieces, outs, sems = refs[:SIDE], refs[SIDE:-1], refs[-1]
    copies = []
    for out, rows in zip(outs, parts):
        for j, part in enumerate(rows):
            for s, piece in enumerate(pieces):
                copies.append(pltpu.make_async_copy(piece.at[part], out.at[j * SIDE + s], sems.at[len(copies)]))
    for copy in copies:
        copy.start()
    for copy in copies:
        copy.wait()


def stack(pieces, *parts):
    return pl.pallas_call(
        functools.partial(stack_kernel, parts),
        in_specs=[VMEM] * SIDE,
        out_specs=[ANY] * len(parts),
        out_shape=[pltpu.HBM((SIDE * len(rows), FT, HD), jnp.bfloat16) for rows in parts],
        scratch_shapes=[pltpu.SemaphoreType.DMA((SIDE * sum(map(len, parts)),))],
        compiler_params=pltpu.CompilerParams(vmem_limit_bytes=LIMIT),
        name="stack",
    )(*pieces)


def block_rows(n):
    return pl.ds(pl.multiple_of(n * BLOCK, BLOCK), BLOCK)


def place(n, keys, values, row, kc, vc, valid=None, stand_in=None):
    ones = lax.broadcasted_iota(jnp.int32, (BLOCK, HD), 1) == 0
    at = slice(n * BLOCK, (n + 1) * BLOCK)
    if valid is None:
        kc[at, :] = keys[block_rows(row), :]
        vc[at, 0:HD] = values[block_rows(row), :]
        vc[at, HD:] = ones.astype(jnp.bfloat16)
    else:
        kc[at, :] = keys[block_rows(jnp.where(valid, row, stand_in)), :]
        taken = values[block_rows(row), :]
        vc[at, 0:HD] = jnp.where(valid, taken, jnp.zeros_like(taken))
        vc[at, HD:] = jnp.where(ones & valid, 1.0, 0.0).astype(jnp.bfloat16)


def band_of(a, b, bs, bw):
    own = a == b
    first = jnp.where(own, 0, bs[a * FRAMES + b])
    second = jnp.where(first == NB - 1, 0, first + 1)
    return first, second, own | (bw[jnp.abs(a - b)] == 2)


def attend_to(q, kc, vc, state, emit):
    kk, vv = kc[...], vc[...]
    steps = FT // ROWS

    def score(r):
        return lax.dot_general(q[r * ROWS : (r + 1) * ROWS, :], kk, NT, preferred_element_type=jnp.float32)

    scores = score(0)
    for r in range(steps):
        later = score(r + 1) if r + 1 < steps else None
        rows = slice(r * ROWS, (r + 1) * ROWS)
        top = jnp.max(scores, axis=1, keepdims=True) * LOG2_SCALE
        if state:
            level = state[1][0, rows, 0:1]
            top = jnp.maximum(top, level)
        probs = jnp.exp2(scores * LOG2_SCALE - top).astype(jnp.bfloat16)
        mixed = lax.dot_general(probs, vv, NN, preferred_element_type=jnp.float32)
        weighted, totals = mixed[:, 0:HD], mixed[:, HD : HD + 1]
        if state:
            share = jnp.exp2(level - top)
            weighted = weighted + state[0][0, rows, :].astype(jnp.float32) * share
            totals = totals + share
        emit(r, (weighted / totals).astype(jnp.bfloat16), top, totals)
        scores = later


def put_state(out, levels):
    def emit(r, result, top, totals):
        rows = slice(r * ROWS, (r + 1) * ROWS)
        out[0, rows, :] = result
        levels[0, rows, :] = jnp.broadcast_to(top + jnp.log2(totals), (ROWS, HD))

    return emit


def put_result(out):
    def emit(r, result, top, totals):
        out[0, r * ROWS : (r + 1) * ROWS, :] = result

    return emit


def line_kernel(qid, kid, bs, bw, q, kv, after, out, levels, kc, vc):
    del after
    i = pl.program_id(0)
    for s in range(SIDE):
        first, second, valid = band_of(qid[i], kid[s], bs, bw)
        place(2 * s, kv.at[s], kv.at[SIDE + s], first, kc, vc)
        place(2 * s + 1, kv.at[s], kv.at[SIDE + s], second, kc, vc, valid, first)
    for j in range(2, NB):
        place(2 * SIDE + j - 2, kv.at[i], kv.at[SIDE + i], j, kc, vc)
    attend_to(q.at[0], kc, vc, None, put_state(out, levels))


def last_line_kernel(qid, kid, bs, bw, q, keys, values, after, out, levels, s1, s2, s3, kc, vc):
    del after
    for s in range(SIDE):
        for i, sent in enumerate((s1, s2, s3)):
            first, second, unused = band_of(qid[i + 1], kid[s], bs, bw)
            for j, source in enumerate((keys, values)):
                sent[s, j, 0:BLOCK, :] = source[s, block_rows(first), :]
                sent[s, j, BLOCK:, :] = source[s, block_rows(second), :]
    for j in range(NB):
        place(j, keys.at[0], values.at[0], j, kc, vc)
    for s in range(1, SIDE):
        first, second, valid = band_of(qid[0], kid[s], bs, bw)
        n = NB + 2 * (s - 1)
        place(n, keys.at[s], values.at[s], first, kc, vc)
        place(n + 1, keys.at[s], values.at[s], second, kc, vc, valid, first)
    attend_to(q, kc, vc, None, put_state(out, levels))


ITEM = pl.BlockSpec((1, FT, HD), lambda i, *_: (i, 0, 0))


def cost(items, blocks):
    pairs_read = items * FT * blocks * BLOCK
    return pl.CostEstimate(flops=pairs_read * 4 * HD, bytes_accessed=8 << 20, transcendentals=pairs_read)


def packed(blocks):
    return [pltpu.VMEM((blocks * BLOCK, HD), jnp.bfloat16), pltpu.VMEM((blocks * BLOCK, 2 * HD), jnp.bfloat16)]


def state_shape(items):
    return [pltpu.HBM((items, FT, HD), jnp.bfloat16), pltpu.HBM((items, FT, HD), jnp.float32)]


def attend_line(qid, kid, bs, bw, q, kv, after):
    blocks = 2 * SIDE + NB - 2
    return pl.pallas_call(
        line_kernel,
        grid_spec=pltpu.PrefetchScalarGridSpec(
            num_scalar_prefetch=4,
            grid=(SIDE,),
            in_specs=[ITEM, pl.BlockSpec(kv.shape, lambda i, *_: (0, 0, 0)), ANY],
            out_specs=[ITEM, ITEM],
            scratch_shapes=packed(blocks),
        ),
        out_shape=state_shape(SIDE),
        compiler_params=pltpu.CompilerParams(vmem_limit_bytes=LIMIT),
        cost_estimate=cost(SIDE, blocks),
        name="attend_line",
    )(qid, kid, bs, bw, *in_hbm(q, kv, after))


def attend_last_line(qid, kid, bs, bw, queries, keys, values, after):
    blocks = 2 * SIDE + NB - 2
    whole = pl.BlockSpec((SIDE, FT, HD), lambda i, *_: (0, 0, 0))
    sent = (SIDE, 2, 2 * BLOCK, HD)
    return pl.pallas_call(
        last_line_kernel,
        grid_spec=pltpu.PrefetchScalarGridSpec(
            num_scalar_prefetch=4,
            grid=(1,),
            in_specs=[pl.BlockSpec((FT, HD), lambda i, *_: (0, SIDE)), whole, whole, ANY],
            out_specs=[ITEM, ITEM] + [pl.BlockSpec(sent, lambda i, *_: (0, 0, 0, 0))] * 3,
            scratch_shapes=packed(blocks),
        ),
        out_shape=state_shape(1) + [pltpu.HBM(sent, jnp.bfloat16)] * 3,
        compiler_params=pltpu.CompilerParams(vmem_limit_bytes=LIMIT),
        cost_estimate=cost(1, blocks),
        name="attend_last_line",
    )(qid, kid, bs, bw, *in_hbm(queries, keys, values, after))


def groups_kernel(count, finished, qid, kid, bs, bw, q, *refs):
    groups, (before, levels), results, (kc, vc) = refs[:count], refs[count : count + 2], refs[count + 2 : -2], refs[-2:]
    i = pl.program_id(0)
    for d, group in enumerate(groups):
        for s in range(SIDE):
            n = d * SIDE + s
            keys, values = group.at[s], group.at[SIDE + s]
            first, second, valid = band_of(qid[i], kid[n], bs, bw)
            place(2 * n, keys, values, first, kc, vc)
            place(2 * n + 1, keys, values, second, kc, vc, valid, first)
    if finished:
        out, token = results
        token[...] = jnp.zeros(token.shape, token.dtype)
        emit = put_result(out)
    else:
        emit = put_state(*results)
    attend_to(q.at[0], kc, vc, (before, levels), emit)


def attend_groups(qid, kid, bs, bw, q, groups, state, finished):
    blocks = 2 * SIDE * len(groups)
    if finished:
        out_specs = [ITEM, pl.BlockSpec((8, HD), lambda i, *_: (0, 0))]
        out_shape = [jax.ShapeDtypeStruct((SIDE, FT, HD), jnp.bfloat16), pltpu.HBM((8, HD), jnp.float32)]
    else:
        out_specs, out_shape = [ITEM, ITEM], state_shape(SIDE)
    return pl.pallas_call(
        functools.partial(groups_kernel, len(groups), finished),
        grid_spec=pltpu.PrefetchScalarGridSpec(
            num_scalar_prefetch=4,
            grid=(SIDE,),
            in_specs=[ITEM] + [pl.BlockSpec(g.shape, lambda i, *_: (0, 0, 0)) for g in groups] + [ITEM, ITEM],
            out_specs=out_specs,
            scratch_shapes=packed(blocks),
        ),
        out_shape=out_shape,
        compiler_params=pltpu.CompilerParams(vmem_limit_bytes=LIMIT),
        cost_estimate=cost(SIDE, blocks),
        name="attend_groups",
    )(qid, kid, bs, bw, *in_hbm(q), *groups, *in_hbm(*state))


def bands_attend_kernel(qid, kid, bs, bw, q, g1, g2, g3, before, levels, after, out, kc, vc):
    del after
    for d, group in enumerate((g1, g2, g3)):
        for s in range(SIDE):
            n = d * SIDE + s
            valid = band_of(qid[0], kid[n], bs, bw)[2]
            place(2 * n, group.at[s, 0], group.at[s, 1], 0, kc, vc)
            place(2 * n + 1, group.at[s, 0], group.at[s, 1], 1, kc, vc, valid, 0)
    attend_to(q, kc, vc, (before, levels), put_result(out))


def attend_bands(qid, kid, bs, bw, queries, groups, state, after):
    blocks = 2 * SIDE * len(groups)
    return pl.pallas_call(
        bands_attend_kernel,
        grid_spec=pltpu.PrefetchScalarGridSpec(
            num_scalar_prefetch=4,
            grid=(1,),
            in_specs=[pl.BlockSpec((FT, HD), lambda i, *_: (0, SIDE))]
            + [pl.BlockSpec(g.shape, lambda i, *_: (0, 0, 0, 0)) for g in groups]
            + [ITEM, ITEM, ANY],
            out_specs=ITEM,
            scratch_shapes=packed(blocks),
        ),
        out_shape=jax.ShapeDtypeStruct((1, FT, HD), jnp.bfloat16),
        compiler_params=pltpu.CompilerParams(vmem_limit_bytes=LIMIT),
        cost_estimate=cost(1, blocks),
        name="attend_bands",
    )(qid, kid, bs, bw, *in_hbm(queries), *groups, *in_hbm(*state, after))


def assemble_kernel(pos, o0, o1, o2, o3, o4, att):
    for s, o in enumerate((o0, o1, o2, o3)):
        head = lax.rem(pos[0] + s, SIDE)
        att[:, pl.ds(pl.multiple_of(head * HD, HD), HD)] = o[...]
    att[:, SIDE * HD :] = o4[...]


def assemble(pos, outs):
    return pl.pallas_call(
        assemble_kernel,
        in_specs=[pl.BlockSpec(memory_space=pltpu.SMEM)] + [VMEM] * 5,
        out_specs=VMEM,
        out_shape=jax.ShapeDtypeStruct((FT, 5 * HD), jnp.bfloat16),
        compiler_params=pltpu.CompilerParams(vmem_limit_bytes=LIMIT),
        name="assemble",
    )(pos, *outs)


def project_kernel(order, blocks, att, att_other, w_mine, w_other, *refs):
    del order, blocks
    out, step = refs[-1], FT // 2
    for r in range(0, FT, step):
        rows = slice(r, r + step)
        total = jnp.dot(att[rows, :], w_mine[...], preferred_element_type=jnp.float32)
        total = total + jnp.dot(att_other[rows, :], w_other[...], preferred_element_type=jnp.float32)
        out[pl.program_id(0), rows, :] = total.astype(jnp.bfloat16)


def project(order, core, att, att_other, weight, other_weight, *after):
    count, width = order.shape[0], weight.shape[1] // 8
    return pl.pallas_call(
        project_kernel,
        grid_spec=pltpu.PrefetchScalarGridSpec(
            num_scalar_prefetch=2,
            grid=(count,),
            in_specs=[
                VMEM,
                VMEM,
                pl.BlockSpec((5 * HD, width), lambda i, order, blocks: (0, blocks[i])),
                pl.BlockSpec((5 * HD, width), lambda i, order, blocks: (0, blocks[i])),
            ]
            + [ANY] * len(after),
            out_specs=VMEM,
        ),
        out_shape=jax.ShapeDtypeStruct((count, FT, width), jnp.bfloat16),
        compiler_params=pltpu.CompilerParams(vmem_limit_bytes=LIMIT),
        name="project",
    )(order, 2 * order + core, att, att_other, *in_hbm(weight, other_weight), *after)


def first_share_kernel(blocks, att, weight, other, base, later):
    del blocks
    base[...] = jnp.dot(att[...], weight[...], preferred_element_type=jnp.float32)
    later[...] = other[...]


def first_share(blocks, att, weight, other_weight):
    width = weight.shape[1] // 8
    block = pl.BlockSpec((5 * HD, width), lambda i, blocks: (0, blocks[0]))
    return pl.pallas_call(
        first_share_kernel,
        grid_spec=pltpu.PrefetchScalarGridSpec(
            num_scalar_prefetch=1, grid=(1,), in_specs=[VMEM, block, block], out_specs=[VMEM] * 2
        ),
        out_shape=[pltpu.VMEM((FT, width), jnp.float32), pltpu.VMEM((5 * HD, width), jnp.bfloat16)],
        compiler_params=pltpu.CompilerParams(vmem_limit_bytes=LIMIT),
        name="first_share",
    )(blocks, att, *in_hbm(weight, other_weight))


def second_share_kernel(att_other, base, weight, out):
    total = base[...] + jnp.dot(att_other[...], weight[...], preferred_element_type=jnp.float32)
    out[...] = total.astype(jnp.bfloat16)


def second_share(att_other, base, weight):
    return pl.pallas_call(
        second_share_kernel,
        in_specs=[VMEM] * 3,
        out_specs=VMEM,
        out_shape=pltpu.VMEM(base.shape, jnp.bfloat16),
        compiler_params=pltpu.CompilerParams(vmem_limit_bytes=LIMIT),
        name="second_share",
    )(att_other, base, weight)


def add(*terms):
    total = terms[0].astype(jnp.float32)
    for t in terms[1:]:
        total = total + t.astype(jnp.float32)
    return total.astype(jnp.bfloat16)


def onward_kernel(near, from_down, from_up, send_up, send_down):
    half = FT // 2
    wide = lambda v: v.astype(jnp.float32)
    send_up[...] = (wide(near[0, 0:half, :]) + wide(from_down[...])).astype(jnp.bfloat16)
    send_down[...] = (wide(near[1, half:, :]) + wide(from_up[...])).astype(jnp.bfloat16)


def onward(near, from_down, from_up):
    return pl.pallas_call(
        onward_kernel,
        in_specs=[VMEM] * 3,
        out_specs=[VMEM] * 2,
        out_shape=[jax.ShapeDtypeStruct(from_up.shape, jnp.bfloat16)] * 2,
        compiler_params=pltpu.CompilerParams(vmem_limit_bytes=LIMIT),
        name="onward",
    )(near, from_down, from_up)


def finish_kernel(own, more_up, plain_up, more_down, plain_down, out):
    half = FT // 2
    wide = lambda v: v.astype(jnp.float32)
    out[0:half, :] = (wide(own[0:half, :]) + wide(more_up[...]) + wide(plain_down[...])).astype(jnp.bfloat16)
    out[half:, :] = (wide(own[half:, :]) + wide(more_down[...]) + wide(plain_up[...])).astype(jnp.bfloat16)


def finish(*args):
    return pl.pallas_call(
        finish_kernel,
        in_specs=[VMEM] * 5,
        out_specs=pl.BlockSpec(args[0].shape, lambda: (0, 0)),
        out_shape=jax.ShapeDtypeStruct(args[0].shape, jnp.bfloat16),
        compiler_params=pltpu.CompilerParams(vmem_limit_bytes=LIMIT),
        name="finish",
    )(*args)


def shards(queries, key_rows, value_rows, out_weight, band_start, band_width):
    frame, head = lax.axis_index("frame"), lax.axis_index("head")
    x, z = frame // SIDE, frame % SIDE
    y, core = head // 2, head % 2
    line = jnp.where(core == 0, z, x)
    ring = jnp.arange(SIDE, dtype=jnp.int32)

    def frames_at(cross, along):
        return jnp.where(
            core == 0,
            (x - cross) % SIDE * SIDE + (z - along) % SIDE,
            (x - along) % SIDE * SIDE + (z - cross) % SIDE,
        )

    f0, f1, f2, f3 = [frames_at(d, ring) for d in range(SIDE)]
    bs, bw = band_start.reshape(-1), band_width

    pieces = pick(line[None], queries, key_rows, value_rows)
    one, three = line_shift(pieces[1], 1), line_shift(pieces[3], 3)
    pieces = [pieces[0], one, line_shift(pieces[2], 2), three]

    other_weight = core_swap(out_weight)

    (kv,) = stack(pieces, (1, 2))
    q, k_last, v_last = stack(pieces, (0,), (3,), (4,))

    groups = [cross_shift(kv, s) for s in range(1, SIDE)]
    state = attend_line(f0, f0, bs, bw, q, kv, other_weight)

    here_and_across = frames_at(-ring, 0)
    *last_state, s_1, s_2, s_3 = attend_last_line(here_and_across, f0, bs, bw, queries, k_last, v_last, state[0])
    last = [cross_shift(sent, s) for s, sent in ((1, s_1), (2, s_2), (3, s_3))]

    state = attend_groups(f0, f1, bs, bw, q, groups[:1], state, False)
    o_main, token = attend_groups(f0, jnp.concatenate([f2, f3]), bs, bw, q, groups[1:], state, True)
    outs = [o_main[0]] + [line_shift(o_main[s], SIDE - s) for s in range(1, SIDE)]
    o_last = attend_bands(frame[None], jnp.concatenate([f1, f2, f3]), bs, bw, queries, last, last_state, token)
    outs.append(o_last[0])

    att = assemble(line[None], outs)
    att_other = core_swap(att)

    def share(ahead, *after):
        order = (y + jnp.array(ahead, jnp.int32)) % SIDE
        return project(order, core, att, att_other, out_weight, other_weight, *after)

    half = FT // 2
    far = (y[None] + 2) % SIDE * 2 + core
    two = second_share(att_other, *first_share(far, att, out_weight, other_weight))
    from_down, from_up = y_shift(two[:half], 1), y_shift(two[half:], 3)
    near = share([1, 3], two)
    plain_up, plain_down = y_shift(near[0, half:], 1), y_shift(near[1, :half], 3)
    send_up, send_down = onward(near, from_down, from_up)
    own = share([0], near)
    return finish(own[0], y_shift(send_up, 1), plain_up, y_shift(send_down, 3), plain_down)


def solution(mesh):
    return jax.shard_map(
        shards,
        mesh=mesh,
        in_specs=(
            P("frame", "head"),
            P("frame", "head"),
            P("frame", "head"),
            P("head", None),
            P(),
            P(),
        ),
        out_specs=P("frame", "head"),
        check_vma=False,
    )
```

```python
import functools

import jax
import jax.numpy as jnp
from jax import lax
from jax.experimental import pallas as pl
from jax.experimental.pallas import tpu as pltpu
from jax.sharding import PartitionSpec as P

HD = 128
BLOCK = 128
NB = 5
FT = 640
FRAMES = 16
SIDE = 4
ROWS = 320
LOG2_SCALE = 1.4426950408889634 / HD**0.5
NT = (((1,), (1,)), ((), ()))
NN = (((1,), (0,)), ((), ()))
BOTH = ("frame", "head")


def pairs(move):
    out = []
    for i in range(128):
        frame, head = divmod(i, 8)
        x, z, y, c = move(*divmod(frame, 4), *divmod(head, 2))
        out.append((i, (x % 4 * 4 + z % 4) * 8 + y % 4 * 2 + c))
    return out


def line_shift(v, s):
    return lax.ppermute(v, BOTH, pairs(lambda x, z, y, c: (x, z + s, y, c) if c == 0 else (x + s, z, y, c)))


def cross_shift(v, s):
    return lax.ppermute(v, BOTH, pairs(lambda x, z, y, c: (x + s, z, y, c) if c == 0 else (x, z + s, y, c)))


def y_shift(v, s):
    return lax.ppermute(v, BOTH, pairs(lambda x, z, y, c: (x, z, y + s, c)))


def core_swap(v):
    return lax.ppermute(v, BOTH, pairs(lambda x, z, y, c: (x, z, y, 1 - c)))


ANY = pl.BlockSpec(memory_space=pl.ANY)
VMEM = pl.BlockSpec(memory_space=pltpu.VMEM)
LIMIT = 20 << 20


def in_hbm(*arrays):
    return [pltpu.with_memory_space_constraint(v, pltpu.HBM) for v in arrays]


def pick_kernel(pos, q_any, k_any, v_any, *refs):
    outs, (q, k, v, sems) = refs[:SIDE], refs[SIDE:]
    rows = FT // 5
    copies = []
    for i in range(5):
        part = pl.ds(i * rows, rows)
        for j, (source, target) in enumerate(((q_any, q), (k_any, k), (v_any, v))):
            copies.append(pltpu.make_async_copy(source.at[part, :], target.at[part, :], sems.at[3 * i + j]))
    for copy in copies:
        copy.start()
    for i in range(5):
        for copy in copies[3 * i : 3 * i + 3]:
            copy.wait()
        part = slice(i * rows, (i + 1) * rows)
        for s, out in enumerate(outs):
            head = lax.rem(pos[0] + s, SIDE)
            columns = pl.ds(pl.multiple_of(head * HD, HD), HD)
            out[0, part, :] = q[part, columns]
            out[1, part, :] = k[part, columns]
            out[2, part, :] = v[part, columns]
            out[3, part, :] = k[part, 4 * HD :]
            out[4, part, :] = v[part, 4 * HD :]


def pick(pos, queries, keys, values):
    return pl.pallas_call(
        pick_kernel,
        in_specs=[pl.BlockSpec(memory_space=pltpu.SMEM)] + [ANY] * 3,
        out_specs=[VMEM] * SIDE,
        out_shape=[pltpu.VMEM((5, FT, HD), jnp.bfloat16)] * SIDE,
        scratch_shapes=[pltpu.VMEM((FT, 5 * HD), jnp.bfloat16)] * 3 + [pltpu.SemaphoreType.DMA((15,))],
        compiler_params=pltpu.CompilerParams(vmem_limit_bytes=LIMIT),
        name="pick",
    )(pos, *in_hbm(queries, keys, values))


HANDED = (0, 2, 1, 3)


def stack_kernel(parts, *refs):
    pieces, outs, sems = refs[:SIDE], refs[SIDE:-1], refs[-1]
    copies = []
    for out, rows in zip(outs, parts):
        for j, part in enumerate(rows):
            for s, piece in zip(HANDED, pieces):
                copies.append(pltpu.make_async_copy(piece.at[part], out.at[j * SIDE + s], sems.at[len(copies)]))
    for copy in copies:
        copy.start()
    for copy in copies:
        copy.wait()


def stack(pieces, *parts):
    return pl.pallas_call(
        functools.partial(stack_kernel, parts),
        in_specs=[VMEM] * SIDE,
        out_specs=[ANY] * len(parts),
        out_shape=[pltpu.HBM((SIDE * len(rows), FT, HD), jnp.bfloat16) for rows in parts],
        scratch_shapes=[pltpu.SemaphoreType.DMA((SIDE * sum(map(len, parts)),))],
        compiler_params=pltpu.CompilerParams(vmem_limit_bytes=LIMIT),
        name="stack",
    )(*[pieces[s] for s in HANDED])


def block_rows(n):
    return pl.ds(pl.multiple_of(n * BLOCK, BLOCK), BLOCK)


def place(n, keys, values, row, kc, vc, valid=None, stand_in=None):
    ones = lax.broadcasted_iota(jnp.int32, (BLOCK, HD), 1) == 0
    at = slice(n * BLOCK, (n + 1) * BLOCK)
    if valid is None:
        kc[at, :] = keys[block_rows(row), :]
        vc[at, 0:HD] = values[block_rows(row), :]
        vc[at, HD:] = ones.astype(jnp.bfloat16)
    else:
        kc[at, :] = keys[block_rows(jnp.where(valid, row, stand_in)), :]
        taken = values[block_rows(row), :]
        vc[at, 0:HD] = jnp.where(valid, taken, jnp.zeros_like(taken))
        vc[at, HD:] = jnp.where(ones & valid, 1.0, 0.0).astype(jnp.bfloat16)


def band_of(a, b, bs, bw):
    own = a == b
    first = jnp.where(own, 0, bs[a * FRAMES + b])
    second = jnp.where(first == NB - 1, 0, first + 1)
    return first, second, own | (bw[jnp.abs(a - b)] == 2)


def attend_to(q, kc, vc, state, emit):
    kk, vv = kc[...], vc[...]
    steps = FT // ROWS

    def score(r):
        return lax.dot_general(q[r * ROWS : (r + 1) * ROWS, :], kk, NT, preferred_element_type=jnp.float32)

    scores = score(0)
    for r in range(steps):
        later = score(r + 1) if r + 1 < steps else None
        rows = slice(r * ROWS, (r + 1) * ROWS)
        top = jnp.max(scores, axis=1, keepdims=True) * LOG2_SCALE
        if state:
            level = state[1][0, rows, 0:1]
            top = jnp.maximum(top, level)
        probs = jnp.exp2(scores * LOG2_SCALE - top).astype(jnp.bfloat16)
        mixed = lax.dot_general(probs, vv, NN, preferred_element_type=jnp.float32)
        weighted, totals = mixed[:, 0:HD], mixed[:, HD : HD + 1]
        if state:
            share = jnp.exp2(level - top)
            weighted = weighted + state[0][0, rows, :].astype(jnp.float32) * share
            totals = totals + share
        emit(r, (weighted / totals).astype(jnp.bfloat16), top, totals)
        scores = later


def put_state(out, levels):
    def emit(r, result, top, totals):
        rows = slice(r * ROWS, (r + 1) * ROWS)
        out[0, rows, :] = result
        levels[0, rows, :] = jnp.broadcast_to(top + jnp.log2(totals), (ROWS, HD))

    return emit


def put_result(out):
    def emit(r, result, top, totals):
        out[0, r * ROWS : (r + 1) * ROWS, :] = result

    return emit


def line_kernel(qid, kid, bs, bw, q, kv, after, out, levels, kc, vc):
    del after
    i = pl.program_id(0)
    for s in range(SIDE):
        first, second, valid = band_of(qid[i], kid[s], bs, bw)
        place(2 * s, kv.at[s], kv.at[SIDE + s], first, kc, vc)
        place(2 * s + 1, kv.at[s], kv.at[SIDE + s], second, kc, vc, valid, first)
    for j in range(2, NB):
        place(2 * SIDE + j - 2, kv.at[i], kv.at[SIDE + i], j, kc, vc)
    attend_to(q.at[0], kc, vc, None, put_state(out, levels))


def last_line_kernel(qid, kid, bs, bw, q, keys, values, after, out, levels, s1, s2, s3, kc, vc):
    del after
    for s in range(SIDE):
        for i, sent in enumerate((s1, s2, s3)):
            first, second, unused = band_of(qid[i + 1], kid[s], bs, bw)
            for j, source in enumerate((keys, values)):
                sent[s, j, 0:BLOCK, :] = source[s, block_rows(first), :]
                sent[s, j, BLOCK:, :] = source[s, block_rows(second), :]
    for j in range(NB):
        place(j, keys.at[0], values.at[0], j, kc, vc)
    for s in range(1, SIDE):
        first, second, valid = band_of(qid[0], kid[s], bs, bw)
        n = NB + 2 * (s - 1)
        place(n, keys.at[s], values.at[s], first, kc, vc)
        place(n + 1, keys.at[s], values.at[s], second, kc, vc, valid, first)
    attend_to(q, kc, vc, None, put_state(out, levels))


ITEM = pl.BlockSpec((1, FT, HD), lambda i, *_: (i, 0, 0))


def cost(items, blocks):
    pairs_read = items * FT * blocks * BLOCK
    return pl.CostEstimate(flops=pairs_read * 4 * HD, bytes_accessed=8 << 20, transcendentals=pairs_read)


def packed(blocks):
    return [pltpu.VMEM((blocks * BLOCK, HD), jnp.bfloat16), pltpu.VMEM((blocks * BLOCK, 2 * HD), jnp.bfloat16)]


def state_shape(items):
    return [pltpu.HBM((items, FT, HD), jnp.bfloat16), pltpu.HBM((items, FT, HD), jnp.float32)]


def attend_line(qid, kid, bs, bw, q, kv, after):
    blocks = 2 * SIDE + NB - 2
    return pl.pallas_call(
        line_kernel,
        grid_spec=pltpu.PrefetchScalarGridSpec(
            num_scalar_prefetch=4,
            grid=(SIDE,),
            in_specs=[ITEM, pl.BlockSpec(kv.shape, lambda i, *_: (0, 0, 0)), ANY],
            out_specs=[ITEM, ITEM],
            scratch_shapes=packed(blocks),
        ),
        out_shape=state_shape(SIDE),
        compiler_params=pltpu.CompilerParams(vmem_limit_bytes=LIMIT),
        cost_estimate=cost(SIDE, blocks),
        name="attend_line",
    )(qid, kid, bs, bw, *in_hbm(q, kv, after))


def attend_last_line(qid, kid, bs, bw, queries, keys, values, after):
    blocks = 2 * SIDE + NB - 2
    whole = pl.BlockSpec((SIDE, FT, HD), lambda i, *_: (0, 0, 0))
    sent = (SIDE, 2, 2 * BLOCK, HD)
    return pl.pallas_call(
        last_line_kernel,
        grid_spec=pltpu.PrefetchScalarGridSpec(
            num_scalar_prefetch=4,
            grid=(1,),
            in_specs=[pl.BlockSpec((FT, HD), lambda i, *_: (0, SIDE)), whole, whole, ANY],
            out_specs=[ITEM, ITEM] + [pl.BlockSpec(sent, lambda i, *_: (0, 0, 0, 0))] * 3,
            scratch_shapes=packed(blocks),
        ),
        out_shape=state_shape(1) + [pltpu.HBM(sent, jnp.bfloat16)] * 3,
        compiler_params=pltpu.CompilerParams(vmem_limit_bytes=LIMIT),
        cost_estimate=cost(1, blocks),
        name="attend_last_line",
    )(qid, kid, bs, bw, *in_hbm(queries, keys, values, after))


def groups_kernel(count, finished, qid, kid, bs, bw, q, *refs):
    groups, (before, levels), results, (kc, vc) = refs[:count], refs[count : count + 2], refs[count + 2 : -2], refs[-2:]
    i = pl.program_id(0)
    for d, group in enumerate(groups):
        for s in range(SIDE):
            n = d * SIDE + s
            keys, values = group.at[s], group.at[SIDE + s]
            first, second, valid = band_of(qid[i], kid[n], bs, bw)
            place(2 * n, keys, values, first, kc, vc)
            place(2 * n + 1, keys, values, second, kc, vc, valid, first)
    if finished:
        out, token = results
        token[...] = jnp.zeros(token.shape, token.dtype)
        emit = put_result(out)
    else:
        emit = put_state(*results)
    attend_to(q.at[0], kc, vc, (before, levels), emit)


def attend_groups(qid, kid, bs, bw, q, groups, state, finished):
    blocks = 2 * SIDE * len(groups)
    if finished:
        out_specs = [ITEM, pl.BlockSpec((8, HD), lambda i, *_: (0, 0))]
        out_shape = [jax.ShapeDtypeStruct((SIDE, FT, HD), jnp.bfloat16), pltpu.HBM((8, HD), jnp.float32)]
    else:
        out_specs, out_shape = [ITEM, ITEM], state_shape(SIDE)
    return pl.pallas_call(
        functools.partial(groups_kernel, len(groups), finished),
        grid_spec=pltpu.PrefetchScalarGridSpec(
            num_scalar_prefetch=4,
            grid=(SIDE,),
            in_specs=[ITEM] + [pl.BlockSpec(g.shape, lambda i, *_: (0, 0, 0)) for g in groups] + [ITEM, ITEM],
            out_specs=out_specs,
            scratch_shapes=packed(blocks),
        ),
        out_shape=out_shape,
        compiler_params=pltpu.CompilerParams(vmem_limit_bytes=LIMIT),
        cost_estimate=cost(SIDE, blocks),
        name="attend_groups",
    )(qid, kid, bs, bw, *in_hbm(q), *groups, *in_hbm(*state))


def bands_attend_kernel(qid, kid, bs, bw, q, g1, g2, g3, before, levels, after, out, kc, vc):
    del after
    for d, group in enumerate((g1, g2, g3)):
        for s in range(SIDE):
            n = d * SIDE + s
            valid = band_of(qid[0], kid[n], bs, bw)[2]
            place(2 * n, group.at[s, 0], group.at[s, 1], 0, kc, vc)
            place(2 * n + 1, group.at[s, 0], group.at[s, 1], 1, kc, vc, valid, 0)
    attend_to(q, kc, vc, (before, levels), put_result(out))


def attend_bands(qid, kid, bs, bw, queries, groups, state, after):
    blocks = 2 * SIDE * len(groups)
    return pl.pallas_call(
        bands_attend_kernel,
        grid_spec=pltpu.PrefetchScalarGridSpec(
            num_scalar_prefetch=4,
            grid=(1,),
            in_specs=[pl.BlockSpec((FT, HD), lambda i, *_: (0, SIDE))]
            + [pl.BlockSpec(g.shape, lambda i, *_: (0, 0, 0, 0)) for g in groups]
            + [ITEM, ITEM, ANY],
            out_specs=ITEM,
            scratch_shapes=packed(blocks),
        ),
        out_shape=jax.ShapeDtypeStruct((1, FT, HD), jnp.bfloat16),
        compiler_params=pltpu.CompilerParams(vmem_limit_bytes=LIMIT),
        cost_estimate=cost(1, blocks),
        name="attend_bands",
    )(qid, kid, bs, bw, *in_hbm(queries), *groups, *in_hbm(*state, after))


def assemble_kernel(pos, o0, o2, o1, o3, o4, att):
    for s, o in zip(HANDED, (o0, o2, o1, o3)):
        head = lax.rem(pos[0] + s, SIDE)
        att[:, pl.ds(pl.multiple_of(head * HD, HD), HD)] = o[...]
    att[:, SIDE * HD :] = o4[...]


def assemble(pos, outs):
    return pl.pallas_call(
        assemble_kernel,
        in_specs=[pl.BlockSpec(memory_space=pltpu.SMEM)] + [VMEM] * 5,
        out_specs=VMEM,
        out_shape=jax.ShapeDtypeStruct((FT, 5 * HD), jnp.bfloat16),
        compiler_params=pltpu.CompilerParams(vmem_limit_bytes=LIMIT),
        name="assemble",
    )(pos, *[outs[s] for s in HANDED], outs[SIDE])


def project_kernel(order, blocks, att, att_other, w_mine, w_other, *refs):
    del order, blocks
    out, step = refs[-1], FT // 2
    for r in range(0, FT, step):
        rows = slice(r, r + step)
        total = jnp.dot(att[rows, :], w_mine[...], preferred_element_type=jnp.float32)
        total = total + jnp.dot(att_other[rows, :], w_other[...], preferred_element_type=jnp.float32)
        out[pl.program_id(0), rows, :] = total.astype(jnp.bfloat16)


def project(order, core, att, att_other, weight, other_weight, *after):
    count, width = order.shape[0], weight.shape[1] // 8
    return pl.pallas_call(
        project_kernel,
        grid_spec=pltpu.PrefetchScalarGridSpec(
            num_scalar_prefetch=2,
            grid=(count,),
            in_specs=[
                VMEM,
                VMEM,
                pl.BlockSpec((5 * HD, width), lambda i, order, blocks: (0, blocks[i])),
                pl.BlockSpec((5 * HD, width), lambda i, order, blocks: (0, blocks[i])),
            ]
            + [ANY] * len(after),
            out_specs=VMEM,
        ),
        out_shape=jax.ShapeDtypeStruct((count, FT, width), jnp.bfloat16),
        compiler_params=pltpu.CompilerParams(vmem_limit_bytes=LIMIT),
        name="project",
    )(order, 2 * order + core, att, att_other, *in_hbm(weight, other_weight), *after)


def first_share_kernel(blocks, att, weight, other, base, later):
    del blocks
    base[...] = jnp.dot(att[...], weight[...], preferred_element_type=jnp.float32)
    later[...] = other[...]


def first_share(blocks, att, weight, other_weight):
    width = weight.shape[1] // 8
    block = pl.BlockSpec((5 * HD, width), lambda i, blocks: (0, blocks[0]))
    return pl.pallas_call(
        first_share_kernel,
        grid_spec=pltpu.PrefetchScalarGridSpec(
            num_scalar_prefetch=1, grid=(1,), in_specs=[VMEM, block, block], out_specs=[VMEM] * 2
        ),
        out_shape=[pltpu.VMEM((FT, width), jnp.float32), pltpu.VMEM((5 * HD, width), jnp.bfloat16)],
        compiler_params=pltpu.CompilerParams(vmem_limit_bytes=LIMIT),
        name="first_share",
    )(blocks, att, *in_hbm(weight, other_weight))


def second_share_kernel(att_other, base, weight, out):
    total = base[...] + jnp.dot(att_other[...], weight[...], preferred_element_type=jnp.float32)
    out[...] = total.astype(jnp.bfloat16)


def second_share(att_other, base, weight):
    return pl.pallas_call(
        second_share_kernel,
        in_specs=[VMEM] * 3,
        out_specs=VMEM,
        out_shape=pltpu.VMEM(base.shape, jnp.bfloat16),
        compiler_params=pltpu.CompilerParams(vmem_limit_bytes=LIMIT),
        name="second_share",
    )(att_other, base, weight)


def add(*terms):
    total = terms[0].astype(jnp.float32)
    for t in terms[1:]:
        total = total + t.astype(jnp.float32)
    return total.astype(jnp.bfloat16)


def onward_kernel(near, from_down, from_up, send_up, send_down):
    half = FT // 2
    wide = lambda v: v.astype(jnp.float32)
    send_up[...] = (wide(near[0, 0:half, :]) + wide(from_down[...])).astype(jnp.bfloat16)
    send_down[...] = (wide(near[1, half:, :]) + wide(from_up[...])).astype(jnp.bfloat16)


def onward(near, from_down, from_up):
    return pl.pallas_call(
        onward_kernel,
        in_specs=[VMEM] * 3,
        out_specs=[VMEM] * 2,
        out_shape=[jax.ShapeDtypeStruct(from_up.shape, jnp.bfloat16)] * 2,
        compiler_params=pltpu.CompilerParams(vmem_limit_bytes=LIMIT),
        name="onward",
    )(near, from_down, from_up)


def finish_kernel(own, more_up, plain_up, more_down, plain_down, out):
    half = FT // 2
    wide = lambda v: v.astype(jnp.float32)
    out[0:half, :] = (wide(own[0:half, :]) + wide(more_up[...]) + wide(plain_down[...])).astype(jnp.bfloat16)
    out[half:, :] = (wide(own[half:, :]) + wide(more_down[...]) + wide(plain_up[...])).astype(jnp.bfloat16)


def finish(*args):
    return pl.pallas_call(
        finish_kernel,
        in_specs=[VMEM] * 5,
        out_specs=pl.BlockSpec(args[0].shape, lambda: (0, 0)),
        out_shape=jax.ShapeDtypeStruct(args[0].shape, jnp.bfloat16),
        compiler_params=pltpu.CompilerParams(vmem_limit_bytes=LIMIT),
        name="finish",
    )(*args)


def shards(queries, key_rows, value_rows, out_weight, band_start, band_width):
    frame, head = lax.axis_index("frame"), lax.axis_index("head")
    x, z = frame // SIDE, frame % SIDE
    y, core = head // 2, head % 2
    line = jnp.where(core == 0, z, x)
    ring = jnp.arange(SIDE, dtype=jnp.int32)

    def frames_at(cross, along):
        return jnp.where(
            core == 0,
            (x - cross) % SIDE * SIDE + (z - along) % SIDE,
            (x - along) % SIDE * SIDE + (z - cross) % SIDE,
        )

    f0, f1, f2, f3 = [frames_at(d, ring) for d in range(SIDE)]
    bs, bw = band_start.reshape(-1), band_width

    pieces = pick(line[None], queries, key_rows, value_rows)
    one, three = line_shift(pieces[1], 1), line_shift(pieces[3], 3)
    pieces = [pieces[0], one, line_shift(pieces[2], 2), three]

    other_weight = core_swap(out_weight)

    (kv,) = stack(pieces, (1, 2))
    q, k_last, v_last = stack(pieces, (0,), (3,), (4,))

    groups = [cross_shift(kv, s) for s in range(1, SIDE)]
    state = attend_line(f0, f0, bs, bw, q, kv, other_weight)

    here_and_across = frames_at(-ring, 0)
    *last_state, s_1, s_2, s_3 = attend_last_line(here_and_across, f0, bs, bw, queries, k_last, v_last, state[0])
    last = [cross_shift(sent, s) for s, sent in ((1, s_1), (2, s_2), (3, s_3))]

    state = attend_groups(f0, f1, bs, bw, q, groups[:1], state, False)
    o_main, token = attend_groups(f0, jnp.concatenate([f2, f3]), bs, bw, q, groups[1:], state, True)
    outs = [o_main[0]] + [line_shift(o_main[s], SIDE - s) for s in range(1, SIDE)]
    o_last = attend_bands(frame[None], jnp.concatenate([f1, f2, f3]), bs, bw, queries, last, last_state, token)
    outs.append(o_last[0])

    att = assemble(line[None], outs)
    att_other = core_swap(att)

    def share(ahead, *after):
        order = (y + jnp.array(ahead, jnp.int32)) % SIDE
        return project(order, core, att, att_other, out_weight, other_weight, *after)

    half = FT // 2
    far = (y[None] + 2) % SIDE * 2 + core
    two = second_share(att_other, *first_share(far, att, out_weight, other_weight))
    from_down, from_up = y_shift(two[:half], 1), y_shift(two[half:], 3)
    near = share([1, 3], two)
    plain_up, plain_down = y_shift(near[0, half:], 1), y_shift(near[1, :half], 3)
    send_up, send_down = onward(near, from_down, from_up)
    own = share([0], near)
    return finish(own[0], y_shift(send_up, 1), plain_up, y_shift(send_down, 3), plain_down)


def solution(mesh):
    return jax.shard_map(
        shards,
        mesh=mesh,
        in_specs=(
            P("frame", "head"),
            P("frame", "head"),
            P("frame", "head"),
            P("head", None),
            P(),
            P(),
        ),
        out_specs=P("frame", "head"),
        check_vma=False,
    )
```
